32 devices in a mesh: grp: 2 (over y), chan: 2 (over x), tm: 4 (over z), pol: 2 (over core).
Axes of the slice: x: 2, y: 2, z: 4, core: 2. Of those that a mesh axis runs over, the one named last changes fastest.
Arguments:
- voltages: bfloat16 [4, 2, 256, 32768], P('grp', 'pol', 'chan', 'tm'), parts along dimension 0, may hold values from -6 to 6
- taps_filter: float32 [16, 2048], replicated, may hold values from -1.5 to 1.5
- tile_a: int32 [14, 64], replicated, may hold values from 0 to 255
- tile_b: int32 [14, 64], replicated, may hold values from 0 to 255
- tile_owner: int32 [14], replicated, may hold values from 0 to 1, as said below
- tile_flags: int32 [14, 16], replicated, may hold values 0 or 1
Outputs:
- visibility: float32 [16, 256, 4, 2, 64, 128], P('pol', ('chan', 'tm'), 'grp'), parts along dimension 2
The draws below stay inside these ranges and needn't reach their ends.
There are 2 independent parts, one for each index of `grp`. The reference program is written for one: setup_inputs(seed, part) draws one part's arguments, and reference() takes and returns one part's arrays. A program takes and returns all parts, laid end to end along the dimension named above; an argument that names none is the same for every part. Nothing has to cross between parts.
Inputs may be any that keep to these rules, and one draw needn't show every extreme that they name: `tile_owner`: one owner holds exactly 8 tiles and the other owner holds all the rest.
All inputs are finite; a program needn't handle non-finite values.
Results may differ from the reference program's by a relative error of at most 0.0035.
Values may be sent and summed in bfloat16 or wider, within the bound.
A program may use at most 128 MiB of HBM per device.

```python
import math
import jax
import jax.numpy as jnp
from jax import lax

S = 256
C = 2048
TAPS = 16
AVG = 8
TS = 64
NTILE = 14
CAP = 8
T_SIZE = 16
GROUPS = 256
N_POL = 2


def draw_tile_owner(key, part):
    heavier = jax.random.randint(jax.random.fold_in(key, 11), (), 0, 2)
    order = jax.random.permutation(jax.random.fold_in(key, 12), NTILE)
    ranked = jnp.where(jnp.arange(NTILE) < CAP, heavier, 1 - heavier)
    return jnp.take(ranked, order).astype(jnp.int32)


def set_ends(drawn, key, least, largest):
    spot = [jax.random.randint(jax.random.fold_in(key, axis), (), 0, length) for axis, length in enumerate(drawn.shape)]
    longest = drawn.shape.index(max(drawn.shape))
    neighbour = spot[:longest] + [(spot[longest] + 1) % drawn.shape[longest]] + spot[longest + 1:]
    return drawn.at[tuple(spot)].set(least).at[tuple(neighbour)].set(largest)


def block_scale(key, extent, shards, smallest, high):
    gain, own = 1.0, jax.random.fold_in(key, 6)
    for axis_at, blocks in shards:
        steps = jnp.exp(jax.random.uniform(jax.random.fold_in(own, axis_at), (blocks,), jnp.float32, smallest / len(shards), high / len(shards)))
        gain = gain * jnp.repeat(steps, extent[axis_at] // blocks).reshape([-1 if axis == axis_at else 1 for axis in range(len(extent))])
    return gain


def noise(own_key, dims, deviation, limit, split=(), held_as=jnp.bfloat16):
    values = deviation * jax.random.normal(own_key, dims, jnp.float32)
    if split:
        values = values * block_scale(own_key, dims, split, -0.22, 0.18)
    return jnp.clip(values, -limit, limit).astype(held_as)


def setup_inputs(seed: int = 0, part: int = 0) -> dict:
    key_of = jax.random.split(jax.random.key(seed), 7)
    part_keys = jax.random.split(jax.random.fold_in(key_of[6], part), 7)
    return {
        "voltages": noise(part_keys[0], (2, 2, S, T_SIZE * C), 1.0, 6.0, ((1, 2), (2, 2), (3, 4))),
        "taps_filter": noise(key_of[1], (TAPS, C), TAPS ** -0.5, 1.5, (), jnp.float32),
        "tile_a": set_ends(jax.random.randint(key_of[2], (NTILE, TS), 0, S), jax.random.fold_in(key_of[2], 1), 0, S - 1).astype(jnp.int32),
        "tile_b": set_ends(jax.random.randint(key_of[3], (NTILE, TS), 0, S), jax.random.fold_in(key_of[3], 1), 0, S - 1).astype(jnp.int32),
        "tile_owner": draw_tile_owner(jax.random.fold_in(key_of[6], 71), part),
        "tile_flags": set_ends((jax.random.randint(key_of[5], (NTILE, T_SIZE), 0, 4) < 3).astype(jnp.int32), jax.random.fold_in(key_of[5], 1), 0, 1),
    }


def station_spectra(samples, taps_filter):
    blocks = samples.astype(jnp.float32).reshape(2, 2, T_SIZE, C)
    padded = jnp.pad(blocks, ((0, 0), (0, 0), (TAPS - 1, 0), (0, 0)))
    filtered = jnp.zeros((2, 2, T_SIZE, C), jnp.float32)
    for tap_index in range(TAPS):
        start = TAPS - 1 - tap_index
        filtered = filtered + taps_filter[tap_index] * padded[:, :, start:start + T_SIZE]
    transformed = jnp.fft.fft(filtered[0] + 1j * filtered[1], axis=-1) / math.sqrt(C)
    return jnp.stack([jnp.real(transformed), jnp.imag(transformed)]).astype(jnp.bfloat16)

def tile_result(arranged, rows_a, rows_b, flags):
    weight = jnp.tile(flags.astype(jnp.bfloat16), AVG)
    left_rows = (jnp.take(arranged, rows_a, axis=2) * weight).astype(jnp.float32)
    right_rows = jnp.take(arranged, rows_b, axis=2).astype(jnp.float32)
    exact_mode = lax.Precision.HIGHEST
    form = 'pank,qbnk->npaqb'
    real_part = jnp.einsum(form, left_rows[0], right_rows[0], precision=exact_mode) + jnp.einsum(form, left_rows[1], right_rows[1], precision=exact_mode)
    imag_part = jnp.einsum(form, left_rows[1], right_rows[0], precision=exact_mode) - jnp.einsum(form, left_rows[0], right_rows[1], precision=exact_mode)
    result = jnp.stack([real_part, imag_part], axis=1) * (1.0 / (AVG * T_SIZE))
    return result.reshape(GROUPS, 2, 2, TS, 2 * TS)

def reference(voltages, taps_filter, tile_a, tile_b, tile_owner, tile_flags):
    by_station = jnp.moveaxis(voltages, 2, 0)
    spectra = lax.map(lambda samples: station_spectra(samples, taps_filter), by_station)
    arranged = spectra.reshape(S, 2, 2, T_SIZE, GROUPS, AVG)
    arranged = arranged.transpose(1, 2, 0, 4, 5, 3).reshape(2, 2, S, GROUPS, AVG * T_SIZE)
    tile_results = lax.map(lambda items: tile_result(arranged, items[0], items[1], items[2]), (tile_a, tile_b, tile_flags))
    slots = []
    for holder in range(N_POL):
        chosen = tile_owner == holder
        listed = jnp.nonzero(chosen, size=CAP, fill_value=0)[0].astype(jnp.int32)
        tally = jnp.sum(chosen.astype(jnp.int32))
        active = jnp.arange(CAP, dtype=jnp.int32) < tally
        picked = jnp.take(tile_results, listed, axis=0)
        slots.append(jnp.where(active[:, None, None, None, None, None], picked, jnp.zeros_like(picked)))
    return jnp.concatenate(slots, axis=0)
```

```python
import functools
import math

import jax
import ml_dtypes
import numpy as np
import jax.numpy as jnp
from jax import lax
from jax.experimental import pallas as pl
from jax.experimental.pallas import tpu as pltpu
from jax.sharding import PartitionSpec as P

AVG = 8
CAP = 8

radix_first = 16
BLOCK = 16
LAST = 0
MESH = pl.DeviceIdType.MESH


def fourier(filtered):
    length = filtered.shape[-1]
    second = length // radix_first
    mode = lax.Precision.HIGH
    grid = filtered.reshape(filtered.shape[:-1] + (radix_first, second))
    outer = jnp.arange(radix_first, dtype=jnp.int32)
    inner = jnp.arange(second, dtype=jnp.int32)
    phase_one = (
        2.0
        * math.pi
        / radix_first
        * (outer[:, None] * outer[None, :] % radix_first).astype(jnp.float32)
    )
    phase_twist = 2.0 * math.pi / length * (outer[:, None] * inner[None, :]).astype(jnp.float32)
    phase_two = (
        2.0 * math.pi / second * (inner[:, None] * inner[None, :] % second).astype(jnp.float32)
    )
    scale = 1.0 / math.sqrt(length)
    cos_one, sin_one = (jnp.cos(phase_one), jnp.sin(phase_one))
    cos_twist, sin_twist = (jnp.cos(phase_twist), jnp.sin(phase_twist))
    cos_two, sin_two = (jnp.cos(phase_two) * scale, jnp.sin(phase_two) * scale)
    one = jnp.stack([jnp.stack([cos_one, sin_one]), jnp.stack([-sin_one, cos_one])])
    two = jnp.stack([jnp.stack([cos_two, sin_two]), jnp.stack([-sin_two, cos_two])])
    section = jnp.einsum("qrfk,rnkj->qnfj", one, grid, precision=mode)
    turned = jnp.stack(
        [
            section[0] * cos_twist + section[1] * sin_twist,
            section[1] * cos_twist - section[0] * sin_twist,
        ]
    )
    return jnp.einsum("qrgj,rnfj->qngf", two, turned, precision=mode)


def times(value, angle):
    re, im = value
    if angle % 16 == 0:
        return re, im
    c, s = math.cos(2.0 * math.pi * angle / 16), math.sin(2.0 * math.pi * angle / 16)
    if angle % 16 == 4:
        return im, -re
    return re * c + im * s, im * c - re * s


def four(x):
    plus = [x[0][i] + x[2][i] for i in range(2)]
    minus = [x[0][i] - x[2][i] for i in range(2)]
    plus_odd = [x[1][i] + x[3][i] for i in range(2)]
    minus_odd = [x[1][i] - x[3][i] for i in range(2)]
    return [
        (plus[0] + plus_odd[0], plus[1] + plus_odd[1]),
        (minus[0] + minus_odd[1], minus[1] - minus_odd[0]),
        (plus[0] - plus_odd[0], plus[1] - plus_odd[1]),
        (minus[0] - minus_odd[1], minus[1] + minus_odd[0]),
    ]


def sixteen(x):
    inner = [four([x[4 * a + b] for a in range(4)]) for b in range(4)]
    result = [None] * 16
    for c in range(4):
        ends = four([times(inner[b][c], b * c) for b in range(4)])
        for d in range(4):
            result[c + 4 * d] = ends[d]
    return result


def filter_and_transform(chunk, got, taps_ref, cos_ref, sin_ref, high_ref, low_ref, made, held, turned):
    time_count, _, _, block, samples_count = got.shape
    taps, length = taps_ref.shape
    frames = samples_count // length
    spectra_count = time_count * frames
    second = length // radix_first
    depth = AVG * spectra_count
    owners, _, units = made.shape[:3]

    def filter_section(k1, carry):
        at = pl.multiple_of(k1 * second, second)
        rows = [taps_ref[m : m + 1, pl.ds(at, second)] for m in range(taps)]
        for r in range(2):
            samples = []
            for t in range(spectra_count):
                place = pl.multiple_of(k1 * second + (t % frames) * length, second)
                samples.append(
                    got[t // frames, chunk, r, :, pl.ds(place, second)].astype(jnp.float32)
                )
            filtered = []
            for t in range(spectra_count):
                total = rows[0] * samples[t]
                for m in range(1, min(taps, t + 1)):
                    total = total + rows[m] * samples[t - m]
                filtered.append(total)
            held[r, :, :, pl.ds(at, second)] = jnp.transpose(jnp.stack(filtered), (1, 0, 2))
        return carry

    lax.fori_loop(0, radix_first, filter_section, 0)

    def transform_station(s, carry):
        sections = [
            tuple(held[r, s, :, k1 * second : (k1 + 1) * second] for r in range(2))
            for k1 in range(radix_first)
        ]
        rows = []
        for f1, (re, im) in enumerate(sixteen(sections)):
            c, n = cos_ref[f1 : f1 + 1, :], sin_ref[f1 : f1 + 1, :]
            rows.append(jnp.concatenate([re * c + im * n, im * c - re * n], axis=-1))
        joined = jnp.concatenate(rows, axis=0)
        high = joined.astype(jnp.bfloat16)
        low = (joined - high.astype(jnp.float32)).astype(jnp.bfloat16)

        def product(matrix, data):
            return lax.dot_general(
                matrix, data, (((1,), (1,)), ((), ())), preferred_element_type=jnp.float32
            )

        turned[s] = (
            product(high_ref[...], high)
            + product(high_ref[...], low)
            + product(low_ref[...], high)
        )
        return carry

    lax.fori_loop(0, block, transform_station, 0)

    def place_channels(o, carry):
        at = pl.multiple_of(o * units, units)
        for q in range(2):
            for h in range(radix_first // AVG):
                part = turned[:, pl.ds(q * second + at, units), h * depth : (h + 1) * depth]
                made[o, chunk, :, h, q] = jnp.transpose(part, (1, 0, 2)).astype(jnp.bfloat16)
        return carry

    lax.fori_loop(0, owners, place_channels, 0)


def exchange_kernel(
    cuts, volt_ref, taps_ref, cos_ref, sin_ref, high_ref, low_ref, *rest
):
    (
        *outs,
        got,
        made,
        held,
        turned,
        local_in,
        send_in,
        recv_in,
        local_out,
        send_out,
        recv_out,
        send_pol,
        recv_pol,
    ) = rest
    own, other = outs[:2]
    later = outs[2] if len(outs) > 2 else None
    times, chunks, _, block, _ = got.shape
    owners, _, units = made.shape[:3]
    inside = own.shape[2]
    chan, tm, pol = lax.axis_index("chan"), lax.axis_index("tm"), lax.axis_index("pol")
    me = chan * times + tm
    pieces = list(zip(cuts[:-1], cuts[1:]))

    def device(k):
        target = lax.rem(me + k, owners)
        return {"chan": target // times, "tm": lax.rem(target, times)}, target

    barrier = pltpu.get_barrier_semaphore()
    for k in range(1, owners):
        pl.semaphore_signal(barrier, inc=1, device_id=device(k)[0], device_id_type=MESH)
    pl.semaphore_signal(barrier, inc=1, device_id={"pol": 1 - pol}, device_id_type=MESH)
    pl.semaphore_wait(barrier, owners)

    def voltages_of(target, chunk):
        at = pl.multiple_of((target * chunks + chunk) * block, block)
        return volt_ref.at[:, pl.ds(at, block), :]

    def copy_in(chunk, d):
        target = lax.rem(tm + d, times)
        return pltpu.make_async_remote_copy(
            src_ref=voltages_of(target, chunk),
            dst_ref=got.at[tm, chunk],
            send_sem=send_in.at[chunk, d - 1],
            recv_sem=recv_in.at[chunk, d - 1],
            device_id={"tm": target},
            device_id_type=MESH,
        )

    def keep_in(chunk):
        return pltpu.make_async_copy(voltages_of(tm, chunk), got.at[tm, chunk], local_in.at[chunk])

    def copy_out(chunk, b, k):
        to, target = device(k)
        span = pl.ds(pieces[b][0], pieces[b][1] - pieces[b][0])
        return pltpu.make_async_remote_copy(
            src_ref=made.at[target, chunk, span],
            dst_ref=own.at[me, chunk, span],
            send_sem=send_out.at[chunk, b, k - 1],
            recv_sem=recv_out.at[chunk, b, k - 1],
            device_id=to,
            device_id_type=MESH,
        )

    def keep_out(chunk):
        return pltpu.make_async_copy(
            made.at[me, chunk, pl.ds(0, inside)], own.at[me, chunk], local_out.at[chunk, 0]
        )

    def keep_later(chunk):
        return pltpu.make_async_copy(
            made.at[:, chunk, pl.ds(inside, units - inside)],
            later.at[:, chunk],
            local_out.at[chunk, 1],
        )

    def copy_pol(chunk, b):
        span = pl.ds(pieces[b][0], pieces[b][1] - pieces[b][0])
        return pltpu.make_async_remote_copy(
            src_ref=own.at[:, chunk, span],
            dst_ref=other.at[:, chunk, span],
            send_sem=send_pol.at[chunk, b],
            recv_sem=recv_pol.at[chunk, b],
            device_id={"pol": 1 - pol},
            device_id_type=MESH,
        )

    for d in range(1, times):
        copy_in(0, d).start()
    for chunk in range(chunks):
        keep_in(chunk).start()
    for chunk in range(1, chunks):
        for d in range(1, times):
            copy_in(chunk - 1, d).wait_send()
            copy_in(chunk, d).start()
    for chunk in range(chunks):
        keep_in(chunk).wait()
        for d in range(1, times):
            copy_in(chunk, d).wait_recv()
        filter_and_transform(
            chunk, got, taps_ref, cos_ref, sin_ref, high_ref, low_ref, made, held, turned
        )
        if chunk == 0:
            for d in range(1, times):
                copy_in(chunks - 1, d).wait_send()
        for b in range(len(pieces)):
            for k in range(1, owners):
                copy_out(chunk, b, k).start()
        keep_out(chunk).start()
        if later is not None:
            keep_later(chunk).start()
    for chunk in range(chunks):
        keep_out(chunk).wait()
        if later is not None:
            keep_later(chunk).wait()
        for b in range(len(pieces)):
            for k in range(1, owners):
                copy_out(chunk, b, k).wait_recv()
            copy_pol(chunk, b).start()
    for chunk in range(chunks):
        for b in range(len(pieces)):
            for k in range(1, owners):
                copy_out(chunk, b, k).wait_send()
            copy_pol(chunk, b).wait()


def exchanged_spectra(voltages, taps_filter, owners, times, last):
    _, stations, samples = voltages.shape
    taps, length = taps_filter.shape
    spectra_count = times * (samples // length)
    second = length // radix_first
    depth = AVG * spectra_count
    halves = radix_first // AVG
    chunks = stations // times // BLOCK
    units = second // owners
    inside = units - last
    inner = np.arange(second)
    twist = 2.0 * np.pi / length * (np.arange(radix_first)[:, None] * inner[None, :])
    phase = 2.0 * np.pi / second * (inner[:, None] * inner[None, :] % second)
    c, s = np.cos(phase) / math.sqrt(length), np.sin(phase) / math.sqrt(length)
    matrix = np.block([[c, s], [-s, c]])
    high = matrix.astype(ml_dtypes.bfloat16)
    low = (matrix - high.astype(np.float64)).astype(ml_dtypes.bfloat16)
    cuts = sorted({0, inside // 3, inside * 2 // 3, inside})
    pieces = len(cuts) - 1
    shape = lambda count: jax.ShapeDtypeStruct(
        (owners, chunks, count, halves, 2, BLOCK, depth), jnp.bfloat16
    )
    outs = [shape(inside)] * 2 + ([shape(last)] if last else [])
    vmem = pl.BlockSpec(memory_space=pltpu.VMEM)
    anywhere = pl.BlockSpec(memory_space=pl.ANY)
    dma = pltpu.SemaphoreType.DMA
    return pl.pallas_call(
        functools.partial(exchange_kernel, cuts),
        in_specs=[anywhere] + [vmem] * 5,
        out_specs=[anywhere] * len(outs),
        out_shape=outs,
        scratch_shapes=[
            pltpu.VMEM((times, chunks, 2, BLOCK, samples), jnp.bfloat16),
            pltpu.VMEM((owners, chunks, units, halves, 2, BLOCK, depth), jnp.bfloat16),
            pltpu.VMEM((2, BLOCK, spectra_count, length), jnp.float32),
            pltpu.VMEM((BLOCK, 2 * second, radix_first * spectra_count), jnp.float32),
            dma((chunks,)),
            dma((chunks, times - 1)),
            dma((chunks, times - 1)),
            dma((chunks, 2)),
            dma((chunks, pieces, owners - 1)),
            dma((chunks, pieces, owners - 1)),
            dma((chunks, pieces)),
            dma((chunks, pieces)),
        ],
        cost_estimate=pl.CostEstimate(
            flops=16 * 10**9, bytes_accessed=32 * 2**20, transcendentals=0
        ),
        compiler_params=pltpu.CompilerParams(
            vmem_limit_bytes=40 * 2**20, collective_id=0, has_side_effects=True
        ),
    )(
        voltages,
        taps_filter,
        np.cos(twist).astype(np.float32),
        np.sin(twist).astype(np.float32),
        high,
        low,
    )


def plain_spectra(blocks, taps_filter):
    _, time_count, share, samples = blocks.shape
    taps, length = taps_filter.shape
    frames = samples // length
    spectra_count = time_count * frames
    blocks = blocks.reshape(2, time_count, share, frames, length)
    blocks = blocks.transpose(0, 2, 1, 3, 4).reshape(2, share, spectra_count, length)
    extended = jnp.pad(blocks, ((0, 0), (0, 0), (taps - 1, 0), (0, 0)))
    filtered = jnp.zeros((2, share, spectra_count, length), jnp.float32)
    for tap_index in range(taps):
        start = taps - 1 - tap_index
        filtered = filtered + taps_filter[tap_index] * extended[
            :, :, start : start + spectra_count
        ].astype(jnp.float32)
    spectra = fourier(filtered.reshape(2, share * spectra_count, length)).astype(jnp.bfloat16)
    outgoing = spectra.reshape(
        2, share, spectra_count, length // radix_first, radix_first // AVG, AVG
    )
    return outgoing.transpose(3, 4, 0, 1, 5, 2).reshape(
        length // radix_first, radix_first // AVG, 2, share, AVG * spectra_count
    )


def correlate_kernel(place_ref, rows_ref, weight_ref, own_ref, other_ref, *rest):
    out_ref, pick, source = rest[-3:]
    sources, chunks, step, halves, parts, block, depth = own_ref.shape
    stations = sources * chunks * block
    capacity = out_ref.shape[0]
    width = out_ref.shape[4]

    @pl.when(pl.program_id(0) == 0)
    def _():
        columns = lax.broadcasted_iota(jnp.int32, pick.shape, 1)
        pick[...] = jnp.where(rows_ref[...] == columns, 1.0, 0.0).astype(jnp.bfloat16)

    for band in range(step * halves):
        for ref, polarisation in ((own_ref, place_ref[0]), (other_ref, 1 - place_ref[0])):
            at = pl.multiple_of(polarisation * (2 * depth), depth)
            source[band, :, pl.ds(at, 2 * depth)] = jnp.concatenate(
                [
                    ref[:, :, band // halves, band % halves, r].reshape(stations, depth)
                    for r in range(2)
                ],
                axis=-1,
            )
        picked = jnp.dot(pick[...], source[band], preferred_element_type=jnp.float32).astype(
            jnp.bfloat16
        )
        for slot in range(capacity):
            at = 2 * width * slot
            weight = weight_ref[slot]
            left = [
                picked[at : at + width, i * depth : (i + 1) * depth] * weight for i in range(4)
            ]
            other = picked[at + width : at + 2 * width]
            left_rows = jnp.concatenate(
                [
                    jnp.concatenate([left[0], left[1]], axis=-1),
                    jnp.concatenate([left[2], left[3]], axis=-1),
                    jnp.concatenate([left[1], -left[0]], axis=-1),
                    jnp.concatenate([left[3], -left[2]], axis=-1),
                ],
                axis=0,
            )
            right_rows = jnp.concatenate([other[:, : 2 * depth], other[:, 2 * depth :]], axis=0)
            result = lax.dot_general(
                left_rows,
                right_rows,
                (((1,), (1,)), ((), ())),
                preferred_element_type=jnp.float32,
            ) * (1.0 / depth)
            out_ref[slot, band] = result.reshape(2, 2, width, 2 * width)


def correlate(place, own, other, rows, weight, total_bands, first, earlier):
    sources, chunks, units, halves, parts, block, depth = own.shape
    width = rows.shape[1] // 2
    step = halves
    given = [] if earlier is None else [earlier]
    piece = pl.BlockSpec(
        (sources, chunks, 1, halves, parts, block, depth), lambda g: (0, 0, g, 0, 0, 0, 0)
    )
    return pl.pallas_call(
        correlate_kernel,
        grid=(units,),
        in_specs=[
            pl.BlockSpec(memory_space=pltpu.SMEM),
            pl.BlockSpec((CAP * 2 * width, 1), lambda g: (0, 0)),
            pl.BlockSpec((CAP, 1, depth), lambda g: (0, 0, 0)),
            piece,
            piece,
        ]
        + [pl.BlockSpec(memory_space=pl.ANY)] * len(given),
        out_specs=pl.BlockSpec(
            (CAP, step, 2, 2, width, 2 * width), lambda g: (0, g + first, 0, 0, 0, 0)
        ),
        out_shape=jax.ShapeDtypeStruct((CAP, total_bands, 2, 2, width, 2 * width), jnp.float32),
        scratch_shapes=[
            pltpu.VMEM((CAP * 2 * width, sources * chunks * block), jnp.bfloat16),
            pltpu.VMEM((step, sources * chunks * block, 4 * depth), jnp.bfloat16),
        ],
        input_output_aliases={5: 0} if given else {},
        cost_estimate=pl.CostEstimate(
            flops=units * 8 * 10**8, bytes_accessed=units * 2**21, transcendentals=0
        ),
        compiler_params=pltpu.CompilerParams(vmem_limit_bytes=48 * 2**20),
    )(
        place,
        rows.reshape(CAP * 2 * width, 1),
        weight.astype(jnp.bfloat16),
        own,
        other,
        *given,
    )


def on_device(voltages, taps_filter, tile_a, tile_b, tile_owner, tile_flags):
    taps, length = taps_filter.shape
    stations = voltages.shape[2]
    frames = voltages.shape[3] // length
    chan_count = lax.axis_size("chan")
    time_count = lax.axis_size("tm")
    spectra_count = time_count * frames
    share = stations // time_count
    owners = chan_count * time_count
    bands = length // (owners * AVG)
    halves = radix_first // AVG

    position = lax.axis_index("pol")
    held = tile_owner == position
    rank = jnp.cumsum(held.astype(jnp.int32)) - 1
    chosen = (
        (rank[None, :] == jnp.arange(CAP, dtype=jnp.int32)[:, None]) & held[None, :]
    ).astype(jnp.int32)
    pairs = jnp.concatenate([tile_a, tile_b], axis=1)
    rows = jnp.sum(chosen[:, :, None] * pairs[None], axis=1)[:, :, None]
    flags = jnp.sum(chosen[:, :, None] * tile_flags[None], axis=1)
    weight = jnp.tile(flags.astype(jnp.float32), (1, AVG))[:, None, :]
    place = position.reshape(1).astype(jnp.int32)
    swap = [(0, 1), (1, 0)]

    if share % BLOCK:
        blocks = voltages.reshape(2, time_count, share, frames * length)
        blocks = lax.all_to_all(blocks, "tm", split_axis=1, concat_axis=1, tiled=True)
        spectra = plain_spectra(blocks, taps_filter)
        outgoing = spectra.reshape(
            owners, 1, bands // halves, halves, 2, share, AVG * spectra_count
        )
        moved = lax.all_to_all(outgoing, ("chan", "tm"), split_axis=0, concat_axis=0, tiled=True)
        other = lax.ppermute(moved, "pol", swap)
        return correlate(place, moved, other, rows, weight, bands, 0, None)

    units = bands // halves
    last = LAST
    own, other, *later = exchanged_spectra(voltages[:, 0], taps_filter, owners, time_count, last)
    if last:
        own_last = lax.all_to_all(
            later[0], ("chan", "tm"), split_axis=0, concat_axis=0, tiled=True
        )
        other_last = lax.ppermute(own_last, "pol", swap)
    visibility = correlate(place, own, other, rows, weight, bands, 0, None)
    if last:
        visibility = correlate(
            place, own_last, other_last, rows, weight, bands, units - last, visibility
        )
    return visibility


def solution(mesh):
    return jax.shard_map(
        on_device,
        mesh=mesh,
        in_specs=(P("grp", "pol", "chan", "tm"), P(), P(), P(), P(), P()),
        out_specs=P("pol", ("chan", "tm"), "grp", None, None, None),
        check_vma=False,
    )
```

```python
import functools
import math

import jax
import ml_dtypes
import numpy as np
import jax.numpy as jnp
from jax import lax
from jax.experimental import pallas as pl
from jax.experimental.pallas import tpu as pltpu
from jax.sharding import PartitionSpec as P

AVG = 8
CAP = 8

radix_first = 16
BLOCK = 16
LAST = 4
PIECES = 7
WINDOW = 2
MESH = pl.DeviceIdType.MESH


def fourier(filtered):
    length = filtered.shape[-1]
    second = length // radix_first
    mode = lax.Precision.HIGH
    grid = filtered.reshape(filtered.shape[:-1] + (radix_first, second))
    outer = jnp.arange(radix_first, dtype=jnp.int32)
    inner = jnp.arange(second, dtype=jnp.int32)
    phase_one = (
        2.0
        * math.pi
        / radix_first
        * (outer[:, None] * outer[None, :] % radix_first).astype(jnp.float32)
    )
    phase_twist = 2.0 * math.pi / length * (outer[:, None] * inner[None, :]).astype(jnp.float32)
    phase_two = (
        2.0 * math.pi / second * (inner[:, None] * inner[None, :] % second).astype(jnp.float32)
    )
    scale = 1.0 / math.sqrt(length)
    cos_one, sin_one = (jnp.cos(phase_one), jnp.sin(phase_one))
    cos_twist, sin_twist = (jnp.cos(phase_twist), jnp.sin(phase_twist))
    cos_two, sin_two = (jnp.cos(phase_two) * scale, jnp.sin(phase_two) * scale)
    one = jnp.stack([jnp.stack([cos_one, sin_one]), jnp.stack([-sin_one, cos_one])])
    two = jnp.stack([jnp.stack([cos_two, sin_two]), jnp.stack([-sin_two, cos_two])])
    section = jnp.einsum("qrfk,rnkj->qnfj", one, grid, precision=mode)
    turned = jnp.stack(
        [
            section[0] * cos_twist + section[1] * sin_twist,
            section[1] * cos_twist - section[0] * sin_twist,
        ]
    )
    return jnp.einsum("qrgj,rnfj->qngf", two, turned, precision=mode)


def times(value, angle):
    re, im = value
    if angle % 16 == 0:
        return re, im
    c, s = math.cos(2.0 * math.pi * angle / 16), math.sin(2.0 * math.pi * angle / 16)
    if angle % 16 == 4:
        return im, -re
    return re * c + im * s, im * c - re * s


def four(x):
    plus = [x[0][i] + x[2][i] for i in range(2)]
    minus = [x[0][i] - x[2][i] for i in range(2)]
    plus_odd = [x[1][i] + x[3][i] for i in range(2)]
    minus_odd = [x[1][i] - x[3][i] for i in range(2)]
    return [
        (plus[0] + plus_odd[0], plus[1] + plus_odd[1]),
        (minus[0] + minus_odd[1], minus[1] - minus_odd[0]),
        (plus[0] - plus_odd[0], plus[1] - plus_odd[1]),
        (minus[0] - minus_odd[1], minus[1] + minus_odd[0]),
    ]


def sixteen(x):
    inner = [four([x[4 * a + b] for a in range(4)]) for b in range(4)]
    result = [None] * 16
    for c in range(4):
        ends = four([times(inner[b][c], b * c) for b in range(4)])
        for d in range(4):
            result[c + 4 * d] = ends[d]
    return result


def filter_and_transform(chunk, got, taps_ref, cos_ref, sin_ref, high_ref, low_ref, made, held, turned):
    time_count, _, _, block, samples_count = got.shape
    taps, length = taps_ref.shape
    frames = samples_count // length
    spectra_count = time_count * frames
    second = length // radix_first
    depth = AVG * spectra_count
    owners, _, units = made.shape[:3]

    def filter_section(k1, carry):
        at = pl.multiple_of(k1 * second, second)
        rows = [taps_ref[m : m + 1, pl.ds(at, second)] for m in range(taps)]
        for r in range(2):
            samples = []
            for t in range(spectra_count):
                place = pl.multiple_of(k1 * second + (t % frames) * length, second)
                samples.append(
                    got[t // frames, chunk, r, :, pl.ds(place, second)].astype(jnp.float32)
                )
            filtered = []
            for t in range(spectra_count):
                total = rows[0] * samples[t]
                for m in range(1, min(taps, t + 1)):
                    total = total + rows[m] * samples[t - m]
                filtered.append(total)
            held[r, :, :, pl.ds(at, second)] = jnp.transpose(jnp.stack(filtered), (1, 0, 2))
        return carry

    lax.fori_loop(0, radix_first, filter_section, 0)

    def transform_station(s, carry):
        sections = [
            tuple(held[r, s, :, k1 * second : (k1 + 1) * second] for r in range(2))
            for k1 in range(radix_first)
        ]
        rows = []
        for f1, (re, im) in enumerate(sixteen(sections)):
            c, n = cos_ref[f1 : f1 + 1, :], sin_ref[f1 : f1 + 1, :]
            rows.append(jnp.concatenate([re * c + im * n, im * c - re * n], axis=-1))
        joined = jnp.concatenate(rows, axis=0)
        high = joined.astype(jnp.bfloat16)
        low = (joined - high.astype(jnp.float32)).astype(jnp.bfloat16)

        def product(matrix, data):
            return lax.dot_general(
                matrix, data, (((1,), (1,)), ((), ())), preferred_element_type=jnp.float32
            )

        turned[s] = (
            product(high_ref[...], high)
            + product(high_ref[...], low)
            + product(low_ref[...], high)
        )
        return carry

    lax.fori_loop(0, block, transform_station, 0)

    def place_channels(o, carry):
        at = pl.multiple_of(o * units, units)
        for q in range(2):
            for h in range(radix_first // AVG):
                part = turned[:, pl.ds(q * second + at, units), h * depth : (h + 1) * depth]
                made[o, chunk, :, h, q] = jnp.transpose(part, (1, 0, 2)).astype(jnp.bfloat16)
        return carry

    lax.fori_loop(0, owners, place_channels, 0)


def choose_tiles(tile_a_ref, tile_b_ref, owner_ref, flags_ref, pick, weight_ref, mine):
    tiles, width = tile_a_ref.shape
    capacity, _, depth = weight_ref.shape
    stations = pick.shape[1]
    held = jnp.where(owner_ref[...] == mine, 1.0, 0.0)
    at = lax.broadcasted_iota(jnp.int32, (tiles, tiles), 0)
    before = lax.broadcasted_iota(jnp.int32, (tiles, tiles), 1)
    held = jnp.broadcast_to(held, (tiles, tiles))
    count = jnp.sum(jnp.where(before <= at, held, 0.0), axis=1, keepdims=True)
    own = jnp.sum(jnp.where(before == at, held, 0.0), axis=1, keepdims=True)
    place = jnp.where(own > 0.5, count - 1.0, -1.0)
    pairs = jnp.concatenate([tile_a_ref[...], tile_b_ref[...]], axis=1).astype(jnp.float32)
    flags = jnp.concatenate(
        [flags_ref[...]] * (depth // flags_ref.shape[1]), axis=1
    ).astype(jnp.float32)
    column = lax.broadcasted_iota(jnp.int32, (2 * width, stations), 1).astype(jnp.float32)
    for slot in range(capacity):
        chosen = jnp.where(place == float(slot), 1.0, 0.0)
        rows = jnp.sum(chosen * pairs, axis=0, keepdims=True)
        rows = jnp.transpose(jnp.broadcast_to(rows, (2 * width, 2 * width)), (1, 0))
        rows = jnp.concatenate([rows] * (stations // (2 * width)), axis=1)
        pick[slot * 2 * width : (slot + 1) * 2 * width, :] = jnp.where(
            rows == column, 1.0, 0.0
        ).astype(jnp.bfloat16)
        weight = jnp.sum(chosen * flags, axis=0, keepdims=True) * (1.0 / depth)
        weight_ref[slot] = weight.astype(jnp.bfloat16)


def correlate_band(first, second, pick, source, weight_ref, out_ref, band):
    depth = weight_ref.shape[2]
    capacity = out_ref.shape[0]
    width = out_ref.shape[4]
    for at, data in enumerate(first + second):
        source[:, at * depth : (at + 1) * depth] = data
    picked = jnp.dot(pick[...], source[...], preferred_element_type=jnp.float32).astype(
        jnp.bfloat16
    )
    for slot in range(capacity):
        at = 2 * width * slot
        weight = weight_ref[slot]
        left = [picked[at : at + width, i * depth : (i + 1) * depth] * weight for i in range(4)]
        other = picked[at + width : at + 2 * width]
        left_rows = jnp.concatenate(
            [
                jnp.concatenate([left[0], left[1]], axis=-1),
                jnp.concatenate([left[2], left[3]], axis=-1),
                jnp.concatenate([left[1], -left[0]], axis=-1),
                jnp.concatenate([left[3], -left[2]], axis=-1),
            ],
            axis=0,
        )
        right_rows = jnp.concatenate([other[:, : 2 * depth], other[:, 2 * depth :]], axis=0)
        result = lax.dot_general(
            left_rows, right_rows, (((1,), (1,)), ((), ())), preferred_element_type=jnp.float32
        )
        out_ref[slot, band] = result.reshape(2, 2, width, 2 * width)


def correlate_unit(unit, own, other, flip, pick, source, weight_ref, out_ref, first_unit=0):
    sources, chunks, _, halves, parts, block, depth = own.shape
    stations = sources * chunks * block
    for half in range(halves):
        mine = [own[:, :, unit, half, r].reshape(stations, depth) for r in range(parts)]
        theirs = [other[:, :, unit, half, r].reshape(stations, depth) for r in range(parts)]
        first = [jnp.where(flip > 0, t, m) for m, t in zip(mine, theirs)]
        second = [jnp.where(flip > 0, m, t) for m, t in zip(mine, theirs)]
        band = (unit - first_unit) * halves + half
        correlate_band(first, second, pick, source.at[half], weight_ref, out_ref, band)


def exchange_kernel(cuts, *refs):
    (
        volt_ref,
        taps_any,
        cos_any,
        sin_any,
        high_any,
        low_any,
        tile_a_any,
        tile_b_any,
        owner_any,
        flags_any,
        own_last,
        other_last,
        pick,
        weight_ref,
        *refs,
    ) = refs
    kept, refs = refs[: len(cuts) - 2], refs[len(cuts) - 2 :]
    (
        got,
        made,
        held,
        turned,
        own,
        other,
        source,
        taps_ref,
        cos_ref,
        sin_ref,
        high_ref,
        low_ref,
        tile_a_ref,
        tile_b_ref,
        owner_ref,
        flags_ref,
        constant_sem,
        local_in,
        send_in,
        recv_in,
        local_out,
        send_out,
        recv_out,
        send_pol,
        recv_pol,
    ) = refs
    times, chunks, _, block, _ = got.shape
    owners, _, units = made.shape[:3]
    inside = own.shape[2]
    chan, tm, pol = lax.axis_index("chan"), lax.axis_index("tm"), lax.axis_index("pol")
    me = chan * times + tm
    pieces = list(zip(cuts[:-1], cuts[1:]))
    count = len(pieces)

    def device(k):
        target = lax.rem(me + k, owners)
        return {"chan": target // times, "tm": lax.rem(target, times)}, target

    barrier = pltpu.get_barrier_semaphore()
    for k in range(1, owners):
        pl.semaphore_signal(barrier, inc=1, device_id=device(k)[0], device_id_type=MESH)
    pl.semaphore_signal(barrier, inc=1, device_id={"pol": 1 - pol}, device_id_type=MESH)
    pl.semaphore_wait(barrier, owners)

    def voltages_of(target, chunk):
        at = pl.multiple_of((target * chunks + chunk) * block, block)
        return volt_ref.at[:, pl.ds(at, block), :]

    def copy_in(chunk, d):
        target = lax.rem(tm + d, times)
        return pltpu.make_async_remote_copy(
            src_ref=voltages_of(target, chunk),
            dst_ref=got.at[tm, chunk],
            send_sem=send_in.at[chunk, d - 1],
            recv_sem=recv_in.at[chunk, d - 1],
            device_id={"tm": target},
            device_id_type=MESH,
        )

    def keep_in(chunk):
        return pltpu.make_async_copy(voltages_of(tm, chunk), got.at[tm, chunk], local_in.at[chunk])

    constants = [
        pltpu.make_async_copy(source_ref, held_ref, constant_sem.at[i])
        for i, (source_ref, held_ref) in enumerate(
            (
                (taps_any, taps_ref),
                (cos_any, cos_ref),
                (sin_any, sin_ref),
                (high_any, high_ref),
                (low_any, low_ref),
                (tile_a_any, tile_a_ref),
                (tile_b_any, tile_b_ref),
                (owner_any, owner_ref),
                (flags_any, flags_ref),
            )
        )
    ]

    def landing(refs, b):
        start, end = pieces[b]
        if start >= inside:
            return refs[1], pl.ds(start - inside, end - start)
        return refs[0], pl.ds(start, end - start)

    def copy_out(chunk, b, k):
        to, target = device(k)
        ref, span = landing((own, own_last), b)
        return pltpu.make_async_remote_copy(
            src_ref=made.at[target, chunk, pl.ds(pieces[b][0], pieces[b][1] - pieces[b][0])],
            dst_ref=ref.at[me, chunk, span],
            send_sem=send_out.at[chunk, b, k - 1],
            recv_sem=recv_out.at[chunk, b, k - 1],
            device_id=to,
            device_id_type=MESH,
        )

    def keep_out(chunk, b):
        ref, span = landing((own, own_last), b)
        return pltpu.make_async_copy(
            made.at[me, chunk, pl.ds(pieces[b][0], pieces[b][1] - pieces[b][0])],
            ref.at[me, chunk, span],
            local_out.at[chunk, b],
        )

    def copy_pol(b):
        ref, span = landing((own, own_last), b)
        target, _ = landing((other, other_last), b)
        return pltpu.make_async_remote_copy(
            src_ref=ref.at[:, :, span],
            dst_ref=target.at[:, :, span],
            send_sem=send_pol.at[b],
            recv_sem=recv_pol.at[b],
            device_id={"pol": 1 - pol},
            device_id_type=MESH,
        )

    def send(chunk, b):
        for k in range(1, owners):
            copy_out(chunk, b, k).start()

    for d in range(1, times):
        copy_in(0, d).start()
    for chunk in range(chunks):
        keep_in(chunk).start()
    for copy in constants:
        copy.start()
    for copy in constants:
        copy.wait()
    choose_tiles(tile_a_ref, tile_b_ref, owner_ref, flags_ref, pick, weight_ref, pol)
    for chunk in range(1, chunks):
        for d in range(1, times):
            copy_in(chunk - 1, d).wait_send()
            copy_in(chunk, d).start()
    for chunk in range(chunks):
        keep_in(chunk).wait()
        for d in range(1, times):
            copy_in(chunk, d).wait_recv()
        filter_and_transform(
            chunk, got, taps_ref, cos_ref, sin_ref, high_ref, low_ref, made, held, turned
        )
        if chunk == 0:
            for d in range(1, times):
                copy_in(chunks - 1, d).wait_send()
        for b in range(count):
            keep_out(chunk, b).start()
            if chunk < chunks - 1 or b < WINDOW:
                send(chunk, b)
    for b in range(count):
        for chunk in range(chunks):
            keep_out(chunk, b).wait()
            for k in range(1, owners):
                copy_out(chunk, b, k).wait_recv()
        copy_pol(b).start()
        if b + WINDOW < count:
            for k in range(1, owners):
                copy_out(chunks - 1, b, k).wait_send()
            send(chunks - 1, b + WINDOW)
        if pieces[b][1] <= inside:
            copy_pol(b).wait_recv()

            def one_unit(unit, carry, b=b):
                correlate_unit(
                    unit, own, other, pol, pick, source, weight_ref, kept[b], pieces[b][0]
                )
                return carry

            lax.fori_loop(pieces[b][0], pieces[b][1], one_unit, 0)
    for b in range(count):
        for chunk in range(chunks):
            if chunk < chunks - 1 or b + WINDOW >= count:
                for k in range(1, owners):
                    copy_out(chunk, b, k).wait_send()
        copy_pol(b).wait_send()
        if pieces[b][0] >= inside:
            copy_pol(b).wait_recv()


def exchange(voltages, taps_filter, tile_a, tile_b, tile_owner, tile_flags, owners, times):
    _, stations, samples = voltages.shape
    taps, length = taps_filter.shape
    spectra_count = times * (samples // length)
    second = length // radix_first
    depth = AVG * spectra_count
    halves = radix_first // AVG
    chunks = stations // times // BLOCK
    units = second // owners
    inside = units - LAST
    tiles, width = tile_a.shape
    inner = np.arange(second)
    twist = 2.0 * np.pi / length * (np.arange(radix_first)[:, None] * inner[None, :])
    phase = 2.0 * np.pi / second * (inner[:, None] * inner[None, :] % second)
    c, s = np.cos(phase) / math.sqrt(length), np.sin(phase) / math.sqrt(length)
    matrix = np.block([[c, s], [-s, c]])
    high = matrix.astype(ml_dtypes.bfloat16)
    low = (matrix - high.astype(np.float64)).astype(ml_dtypes.bfloat16)
    cuts = [inside * i // (PIECES - 1) for i in range(PIECES)] + [units]
    shape = lambda count: (owners, chunks, count, halves, 2, BLOCK, depth)
    vmem = pl.BlockSpec(memory_space=pltpu.VMEM)
    anywhere = pl.BlockSpec(memory_space=pl.ANY)
    dma = pltpu.SemaphoreType.DMA
    far = lambda value: pltpu.with_memory_space_constraint(jnp.asarray(value), pltpu.HBM)
    return pl.pallas_call(
        functools.partial(exchange_kernel, cuts),
        in_specs=[pl.BlockSpec(memory_space=pltpu.HBM)] * 10,
        out_specs=[anywhere] * 2 + [vmem] * (1 + PIECES),
        out_shape=[
            jax.ShapeDtypeStruct(shape(LAST), jnp.bfloat16),
            jax.ShapeDtypeStruct(shape(LAST), jnp.bfloat16),
            jax.ShapeDtypeStruct((CAP * 2 * width, owners * chunks * BLOCK), jnp.bfloat16),
            jax.ShapeDtypeStruct((CAP, 1, depth), jnp.bfloat16),
        ]
        + [
            jax.ShapeDtypeStruct((CAP, (end - start) * halves, 2, 2, width, 2 * width), jnp.float32)
            for start, end in zip(cuts[:-2], cuts[1:-1])
        ],
        scratch_shapes=[
            pltpu.VMEM((times, chunks, 2, BLOCK, samples), jnp.bfloat16),
            pltpu.VMEM(shape(units), jnp.bfloat16),
            pltpu.VMEM((2, BLOCK, spectra_count, length), jnp.float32),
            pltpu.VMEM((BLOCK, 2 * second, radix_first * spectra_count), jnp.float32),
            pltpu.VMEM(shape(inside), jnp.bfloat16),
            pltpu.VMEM(shape(inside), jnp.bfloat16),
            pltpu.VMEM((halves, owners * chunks * BLOCK, 4 * depth), jnp.bfloat16),
            pltpu.VMEM((taps, length), jnp.float32),
            pltpu.VMEM((radix_first, second), jnp.float32),
            pltpu.VMEM((radix_first, second), jnp.float32),
            pltpu.VMEM((2 * second, 2 * second), jnp.bfloat16),
            pltpu.VMEM((2 * second, 2 * second), jnp.bfloat16),
            pltpu.VMEM((tiles, width), jnp.int32),
            pltpu.VMEM((tiles, width), jnp.int32),
            pltpu.VMEM((1, tiles), jnp.int32),
            pltpu.VMEM(tile_flags.shape, jnp.int32),
            dma((9,)),
            dma((chunks,)),
            dma((chunks, times - 1)),
            dma((chunks, times - 1)),
            dma((chunks, PIECES)),
            dma((chunks, PIECES, owners - 1)),
            dma((chunks, PIECES, owners - 1)),
            dma((PIECES,)),
            dma((PIECES,)),
        ],
        cost_estimate=pl.CostEstimate(
            flops=16 * 10**9, bytes_accessed=32 * 2**20, transcendentals=0
        ),
        compiler_params=pltpu.CompilerParams(
            vmem_limit_bytes=24 * 2**20, collective_id=0, has_side_effects=True
        ),
    )(
        voltages,
        far(taps_filter),
        far(np.cos(twist).astype(np.float32)),
        far(np.sin(twist).astype(np.float32)),
        far(high),
        far(low),
        far(tile_a),
        far(tile_b),
        far(tile_owner.reshape(1, tiles)),
        far(tile_flags),
    )


def finish_kernel(own, other, pick, weight_ref, *refs):
    *kept, out_ref, source, block, kept_sem, block_sem = refs
    units, halves = own.shape[2:4]
    pol = lax.axis_index("pol")
    copies, inside = [], 0
    for i, vis in enumerate(kept):
        bands = vis.shape[1]
        copies.append(
            pltpu.make_async_copy(vis, out_ref.at[:, pl.ds(inside, bands)], kept_sem.at[i])
        )
        inside += bands
    for copy in copies:
        copy.start()
    for unit in range(units):
        correlate_unit(unit, own, other, pol, pick, source, weight_ref, block)
        copy = pltpu.make_async_copy(
            block.at[:, pl.ds(unit * halves, halves)],
            out_ref.at[:, pl.ds(inside + unit * halves, halves)],
            block_sem.at[unit],
        )
        copy.start()
        copies.append(copy)
    for copy in copies:
        copy.wait()


def finish(own, other, pick, weight, *kept):
    capacity = kept[0].shape[0]
    inside = sum(vis.shape[1] for vis in kept)
    sources, chunks, units, halves, _, block, depth = own.shape
    rest = kept[0].shape[2:]
    vmem = pl.BlockSpec(memory_space=pltpu.VMEM)
    return pl.pallas_call(
        finish_kernel,
        in_specs=[vmem] * (4 + len(kept)),
        out_specs=pl.BlockSpec(memory_space=pl.ANY),
        out_shape=jax.ShapeDtypeStruct((capacity, inside + units * halves) + rest, jnp.float32),
        scratch_shapes=[
            pltpu.VMEM((halves, sources * chunks * block, 4 * depth), jnp.bfloat16),
            pltpu.VMEM((capacity, units * halves) + rest, jnp.float32),
            pltpu.SemaphoreType.DMA((len(kept),)),
            pltpu.SemaphoreType.DMA((units,)),
        ],
        compiler_params=pltpu.CompilerParams(vmem_limit_bytes=14 * 2**20),
    )(own, other, pick, weight, *kept)


def plain_spectra(blocks, taps_filter):
    _, time_count, share, samples = blocks.shape
    taps, length = taps_filter.shape
    frames = samples // length
    spectra_count = time_count * frames
    blocks = blocks.reshape(2, time_count, share, frames, length)
    blocks = blocks.transpose(0, 2, 1, 3, 4).reshape(2, share, spectra_count, length)
    extended = jnp.pad(blocks, ((0, 0), (0, 0), (taps - 1, 0), (0, 0)))
    filtered = jnp.zeros((2, share, spectra_count, length), jnp.float32)
    for tap_index in range(taps):
        start = taps - 1 - tap_index
        filtered = filtered + taps_filter[tap_index] * extended[
            :, :, start : start + spectra_count
        ].astype(jnp.float32)
    spectra = fourier(filtered.reshape(2, share * spectra_count, length)).astype(jnp.bfloat16)
    outgoing = spectra.reshape(
        2, share, spectra_count, length // radix_first, radix_first // AVG, AVG
    )
    return outgoing.transpose(3, 4, 0, 1, 5, 2).reshape(
        length // radix_first, radix_first // AVG, 2, share, AVG * spectra_count
    )


def correlate_kernel(place_ref, rows_ref, weight_ref, own_ref, other_ref, *rest):
    out_ref, pick, source = rest[-3:]
    sources, chunks, step, halves, parts, block, depth = own_ref.shape
    stations = sources * chunks * block
    capacity = out_ref.shape[0]
    width = out_ref.shape[4]

    @pl.when(pl.program_id(0) == 0)
    def _():
        columns = lax.broadcasted_iota(jnp.int32, pick.shape, 1)
        pick[...] = jnp.where(rows_ref[...] == columns, 1.0, 0.0).astype(jnp.bfloat16)

    for band in range(step * halves):
        for ref, polarisation in ((own_ref, place_ref[0]), (other_ref, 1 - place_ref[0])):
            at = pl.multiple_of(polarisation * (2 * depth), depth)
            source[band, :, pl.ds(at, 2 * depth)] = jnp.concatenate(
                [
                    ref[:, :, band // halves, band % halves, r].reshape(stations, depth)
                    for r in range(2)
                ],
                axis=-1,
            )
        picked = jnp.dot(pick[...], source[band], preferred_element_type=jnp.float32).astype(
            jnp.bfloat16
        )
        for slot in range(capacity):
            at = 2 * width * slot
            weight = weight_ref[slot]
            left = [
                picked[at : at + width, i * depth : (i + 1) * depth] * weight for i in range(4)
            ]
            other = picked[at + width : at + 2 * width]
            left_rows = jnp.concatenate(
                [
                    jnp.concatenate([left[0], left[1]], axis=-1),
                    jnp.concatenate([left[2], left[3]], axis=-1),
                    jnp.concatenate([left[1], -left[0]], axis=-1),
                    jnp.concatenate([left[3], -left[2]], axis=-1),
                ],
                axis=0,
            )
            right_rows = jnp.concatenate([other[:, : 2 * depth], other[:, 2 * depth :]], axis=0)
            result = lax.dot_general(
                left_rows,
                right_rows,
                (((1,), (1,)), ((), ())),
                preferred_element_type=jnp.float32,
            ) * (1.0 / depth)
            out_ref[slot, band] = result.reshape(2, 2, width, 2 * width)


def correlate(place, own, other, rows, weight, total_bands, first, earlier):
    sources, chunks, units, halves, parts, block, depth = own.shape
    width = rows.shape[1] // 2
    step = halves
    given = [] if earlier is None else [earlier]
    piece = pl.BlockSpec(
        (sources, chunks, 1, halves, parts, block, depth), lambda g: (0, 0, g, 0, 0, 0, 0)
    )
    return pl.pallas_call(
        correlate_kernel,
        grid=(units,),
        in_specs=[
            pl.BlockSpec(memory_space=pltpu.SMEM),
            pl.BlockSpec((CAP * 2 * width, 1), lambda g: (0, 0)),
            pl.BlockSpec((CAP, 1, depth), lambda g: (0, 0, 0)),
            piece,
            piece,
        ]
        + [pl.BlockSpec(memory_space=pl.ANY)] * len(given),
        out_specs=pl.BlockSpec(
            (CAP, step, 2, 2, width, 2 * width), lambda g: (0, g + first, 0, 0, 0, 0)
        ),
        out_shape=jax.ShapeDtypeStruct((CAP, total_bands, 2, 2, width, 2 * width), jnp.float32),
        scratch_shapes=[
            pltpu.VMEM((CAP * 2 * width, sources * chunks * block), jnp.bfloat16),
            pltpu.VMEM((step, sources * chunks * block, 4 * depth), jnp.bfloat16),
        ],
        input_output_aliases={5: 0} if given else {},
        cost_estimate=pl.CostEstimate(
            flops=units * 8 * 10**8, bytes_accessed=units * 2**21, transcendentals=0
        ),
        compiler_params=pltpu.CompilerParams(vmem_limit_bytes=48 * 2**20),
    )(
        place,
        rows.reshape(CAP * 2 * width, 1),
        weight.astype(jnp.bfloat16),
        own,
        other,
        *given,
    )


def on_device(voltages, taps_filter, tile_a, tile_b, tile_owner, tile_flags):
    taps, length = taps_filter.shape
    stations = voltages.shape[2]
    frames = voltages.shape[3] // length
    chan_count = lax.axis_size("chan")
    time_count = lax.axis_size("tm")
    spectra_count = time_count * frames
    share = stations // time_count
    owners = chan_count * time_count
    bands = length // (owners * AVG)
    halves = radix_first // AVG

    if share % BLOCK == 0:
        results = exchange(
            voltages[:, 0],
            taps_filter,
            tile_a,
            tile_b,
            tile_owner,
            tile_flags,
            owners,
            time_count,
        )
        return finish(*results)

    position = lax.axis_index("pol")
    held = tile_owner == position
    rank = jnp.cumsum(held.astype(jnp.int32)) - 1
    chosen = (
        (rank[None, :] == jnp.arange(CAP, dtype=jnp.int32)[:, None]) & held[None, :]
    ).astype(jnp.int32)
    pairs = jnp.concatenate([tile_a, tile_b], axis=1)
    rows = jnp.sum(chosen[:, :, None] * pairs[None], axis=1)[:, :, None]
    flags = jnp.sum(chosen[:, :, None] * tile_flags[None], axis=1)
    weight = jnp.tile(flags.astype(jnp.float32), (1, AVG))[:, None, :]
    place = position.reshape(1).astype(jnp.int32)
    swap = [(0, 1), (1, 0)]

    blocks = voltages.reshape(2, time_count, share, frames * length)
    blocks = lax.all_to_all(blocks, "tm", split_axis=1, concat_axis=1, tiled=True)
    spectra = plain_spectra(blocks, taps_filter)
    outgoing = spectra.reshape(owners, 1, bands // halves, halves, 2, share, AVG * spectra_count)
    moved = lax.all_to_all(outgoing, ("chan", "tm"), split_axis=0, concat_axis=0, tiled=True)
    other = lax.ppermute(moved, "pol", swap)
    return correlate(place, moved, other, rows, weight, bands, 0, None)


def solution(mesh):
    return jax.shard_map(
        on_device,
        mesh=mesh,
        in_specs=(P("grp", "pol", "chan", "tm"), P(), P(), P(), P(), P()),
        out_specs=P("pol", ("chan", "tm"), "grp", None, None, None),
        check_vma=False,
    )
```

```python
import functools
import math

import jax
import ml_dtypes
import numpy as np
import jax.numpy as jnp
from jax import lax
from jax.experimental import pallas as pl
from jax.experimental.pallas import tpu as pltpu
from jax.sharding import PartitionSpec as P

AVG = 8
CAP = 8

radix_first = 16
BLOCK = 16
LAST = 6
KEEP = 2
WINDOW = 3
MESH = pl.DeviceIdType.MESH


def fourier(filtered):
    length = filtered.shape[-1]
    second = length // radix_first
    mode = lax.Precision.HIGH
    grid = filtered.reshape(filtered.shape[:-1] + (radix_first, second))
    outer = jnp.arange(radix_first, dtype=jnp.int32)
    inner = jnp.arange(second, dtype=jnp.int32)
    phase_one = (
        2.0
        * math.pi
        / radix_first
        * (outer[:, None] * outer[None, :] % radix_first).astype(jnp.float32)
    )
    phase_twist = 2.0 * math.pi / length * (outer[:, None] * inner[None, :]).astype(jnp.float32)
    phase_two = (
        2.0 * math.pi / second * (inner[:, None] * inner[None, :] % second).astype(jnp.float32)
    )
    scale = 1.0 / math.sqrt(length)
    cos_one, sin_one = (jnp.cos(phase_one), jnp.sin(phase_one))
    cos_twist, sin_twist = (jnp.cos(phase_twist), jnp.sin(phase_twist))
    cos_two, sin_two = (jnp.cos(phase_two) * scale, jnp.sin(phase_two) * scale)
    one = jnp.stack([jnp.stack([cos_one, sin_one]), jnp.stack([-sin_one, cos_one])])
    two = jnp.stack([jnp.stack([cos_two, sin_two]), jnp.stack([-sin_two, cos_two])])
    section = jnp.einsum("qrfk,rnkj->qnfj", one, grid, precision=mode)
    turned = jnp.stack(
        [
            section[0] * cos_twist + section[1] * sin_twist,
            section[1] * cos_twist - section[0] * sin_twist,
        ]
    )
    return jnp.einsum("qrgj,rnfj->qngf", two, turned, precision=mode)


def times(value, angle):
    re, im = value
    if angle % 16 == 0:
        return re, im
    c, s = math.cos(2.0 * math.pi * angle / 16), math.sin(2.0 * math.pi * angle / 16)
    if angle % 16 == 4:
        return im, -re
    return re * c + im * s, im * c - re * s


def four(x):
    plus = [x[0][i] + x[2][i] for i in range(2)]
    minus = [x[0][i] - x[2][i] for i in range(2)]
    plus_odd = [x[1][i] + x[3][i] for i in range(2)]
    minus_odd = [x[1][i] - x[3][i] for i in range(2)]
    return [
        (plus[0] + plus_odd[0], plus[1] + plus_odd[1]),
        (minus[0] + minus_odd[1], minus[1] - minus_odd[0]),
        (plus[0] - plus_odd[0], plus[1] - plus_odd[1]),
        (minus[0] - minus_odd[1], minus[1] + minus_odd[0]),
    ]


def sixteen(x):
    inner = [four([x[4 * a + b] for a in range(4)]) for b in range(4)]
    result = [None] * 16
    for c in range(4):
        ends = four([times(inner[b][c], b * c) for b in range(4)])
        for d in range(4):
            result[c + 4 * d] = ends[d]
    return result


def filter_and_transform(chunk, got, taps_ref, cos_ref, sin_ref, high_ref, low_ref, made, held, turned):
    time_count, _, _, block, samples_count = got.shape
    taps, length = taps_ref.shape
    frames = samples_count // length
    spectra_count = time_count * frames
    second = length // radix_first
    depth = AVG * spectra_count
    owners, _, units = made.shape[:3]

    def filter_section(k1, carry):
        at = pl.multiple_of(k1 * second, second)
        rows = [taps_ref[m : m + 1, pl.ds(at, second)] for m in range(taps)]
        for r in range(2):
            samples = []
            for t in range(spectra_count):
                place = pl.multiple_of(k1 * second + (t % frames) * length, second)
                samples.append(
                    got[t // frames, chunk, r, :, pl.ds(place, second)].astype(jnp.float32)
                )
            filtered = []
            for t in range(spectra_count):
                total = rows[0] * samples[t]
                for m in range(1, min(taps, t + 1)):
                    total = total + rows[m] * samples[t - m]
                filtered.append(total)
            held[r, :, :, pl.ds(at, second)] = jnp.transpose(jnp.stack(filtered), (1, 0, 2))
        return carry

    lax.fori_loop(0, radix_first, filter_section, 0)

    def transform_station(s, carry):
        sections = [
            tuple(held[r, s, :, k1 * second : (k1 + 1) * second] for r in range(2))
            for k1 in range(radix_first)
        ]
        rows = []
        for f1, (re, im) in enumerate(sixteen(sections)):
            c, n = cos_ref[f1 : f1 + 1, :], sin_ref[f1 : f1 + 1, :]
            rows.append(jnp.concatenate([re * c + im * n, im * c - re * n], axis=-1))
        joined = jnp.concatenate(rows, axis=0)
        high = joined.astype(jnp.bfloat16)
        low = (joined - high.astype(jnp.float32)).astype(jnp.bfloat16)

        def product(matrix, data):
            return lax.dot_general(
                matrix, data, (((1,), (1,)), ((), ())), preferred_element_type=jnp.float32
            )

        turned[s] = (
            product(high_ref[...], high)
            + product(high_ref[...], low)
            + product(low_ref[...], high)
        )
        return carry

    lax.fori_loop(0, block, transform_station, 0)

    def place_channels(o, carry):
        at = pl.multiple_of(o * units, units)
        for q in range(2):
            for h in range(radix_first // AVG):
                part = turned[:, pl.ds(q * second + at, units), h * depth : (h + 1) * depth]
                made[o, chunk, :, h, q] = jnp.transpose(part, (1, 0, 2)).astype(jnp.bfloat16)
        return carry

    lax.fori_loop(0, owners, place_channels, 0)


def choose_tiles(tile_a_ref, tile_b_ref, owner_ref, flags_ref, pick, weight_ref, mine):
    tiles, width = tile_a_ref.shape
    capacity, _, depth = weight_ref.shape
    stations = pick.shape[1]
    held = jnp.where(owner_ref[...] == mine, 1.0, 0.0)
    at = lax.broadcasted_iota(jnp.int32, (tiles, tiles), 0)
    before = lax.broadcasted_iota(jnp.int32, (tiles, tiles), 1)
    held = jnp.broadcast_to(held, (tiles, tiles))
    count = jnp.sum(jnp.where(before <= at, held, 0.0), axis=1, keepdims=True)
    own = jnp.sum(jnp.where(before == at, held, 0.0), axis=1, keepdims=True)
    place = jnp.where(own > 0.5, count - 1.0, -1.0)
    pairs = jnp.concatenate([tile_a_ref[...], tile_b_ref[...]], axis=1).astype(jnp.float32)
    flags = jnp.concatenate(
        [flags_ref[...]] * (depth // flags_ref.shape[1]), axis=1
    ).astype(jnp.float32)
    column = lax.broadcasted_iota(jnp.int32, (2 * width, stations), 1).astype(jnp.float32)
    for slot in range(capacity):
        chosen = jnp.where(place == float(slot), 1.0, 0.0)
        rows = jnp.sum(chosen * pairs, axis=0, keepdims=True)
        rows = jnp.transpose(jnp.broadcast_to(rows, (2 * width, 2 * width)), (1, 0))
        rows = jnp.concatenate([rows] * (stations // (2 * width)), axis=1)
        pick[slot * 2 * width : (slot + 1) * 2 * width, :] = jnp.where(
            rows == column, 1.0, 0.0
        ).astype(jnp.bfloat16)
        weight = jnp.sum(chosen * flags, axis=0, keepdims=True) * (1.0 / depth)
        weight_ref[slot] = weight.astype(jnp.bfloat16)


def correlate_band(first, second, pick, weight_ref, out_ref, band):
    depth = weight_ref.shape[2]
    capacity = out_ref.shape[0]
    width = out_ref.shape[4]
    data = jnp.concatenate(first + second, axis=-1)
    picked = jnp.dot(pick[...], data, preferred_element_type=jnp.float32).astype(jnp.bfloat16)
    for slot in range(capacity):
        at = 2 * width * slot
        weight = weight_ref[slot]
        left = [picked[at : at + width, i * depth : (i + 1) * depth] * weight for i in range(4)]
        other = picked[at + width : at + 2 * width]
        left_rows = jnp.concatenate(
            [
                jnp.concatenate([left[0], left[1]], axis=-1),
                jnp.concatenate([left[2], left[3]], axis=-1),
                jnp.concatenate([left[1], -left[0]], axis=-1),
                jnp.concatenate([left[3], -left[2]], axis=-1),
            ],
            axis=0,
        )
        right_rows = jnp.concatenate([other[:, : 2 * depth], other[:, 2 * depth :]], axis=0)
        result = lax.dot_general(
            left_rows, right_rows, (((1,), (1,)), ((), ())), preferred_element_type=jnp.float32
        )
        out_ref[slot, band] = result.reshape(2, 2, width, 2 * width)


def correlate_unit(unit, own, other, flip, pick, weight_ref, out_ref, first_unit=0):
    sources, chunks, _, halves, parts, block, depth = own.shape
    stations = sources * chunks * block
    for half in range(halves):
        mine = [own[:, :, unit, half, r].reshape(stations, depth) for r in range(parts)]
        theirs = [other[:, :, unit, half, r].reshape(stations, depth) for r in range(parts)]
        first = [jnp.where(flip > 0, t, m) for m, t in zip(mine, theirs)]
        second = [jnp.where(flip > 0, m, t) for m, t in zip(mine, theirs)]
        band = (unit - first_unit) * halves + half
        correlate_band(first, second, pick, weight_ref, out_ref, band)


def exchange_kernel(early_cuts, late_cuts, *refs):
    (
        volt_ref,
        taps_any,
        cos_any,
        sin_any,
        high_any,
        low_any,
        tile_a_any,
        tile_b_any,
        owner_any,
        flags_any,
        own_last,
        other_last,
        pick,
        weight_ref,
        *refs,
    ) = refs
    kept, refs = refs[:-24], refs[-24:]
    (
        got,
        made,
        held,
        turned,
        own,
        other,
        taps_ref,
        cos_ref,
        sin_ref,
        high_ref,
        low_ref,
        tile_a_ref,
        tile_b_ref,
        owner_ref,
        flags_ref,
        constant_sem,
        local_in,
        send_in,
        recv_in,
        local_out,
        send_out,
        recv_out,
        send_pol,
        recv_pol,
    ) = refs
    times, chunks, _, block, _ = got.shape
    owners, _, units = made.shape[:3]
    inside = own.shape[2]
    chan, tm, pol = lax.axis_index("chan"), lax.axis_index("tm"), lax.axis_index("pol")
    me = chan * times + tm
    spans = lambda cuts: list(zip(cuts[:-1], cuts[1:]))
    pieces = [spans(early_cuts)] * (chunks - 1) + [spans(late_cuts)]
    lately = chunks - 1
    count = len(pieces[lately])

    def device(k):
        target = lax.rem(me + k, owners)
        return {"chan": target // times, "tm": lax.rem(target, times)}, target

    barrier = pltpu.get_barrier_semaphore()
    for k in range(1, owners):
        pl.semaphore_signal(barrier, inc=1, device_id=device(k)[0], device_id_type=MESH)
    pl.semaphore_signal(barrier, inc=1, device_id={"pol": 1 - pol}, device_id_type=MESH)
    pl.semaphore_wait(barrier, owners)

    def voltages_of(target, chunk):
        at = pl.multiple_of((target * chunks + chunk) * block, block)
        return volt_ref.at[:, pl.ds(at, block), :]

    def copy_in(chunk, r, d):
        target = lax.rem(tm + d, times)
        return pltpu.make_async_remote_copy(
            src_ref=voltages_of(target, chunk).at[r],
            dst_ref=got.at[tm, chunk, r],
            send_sem=send_in.at[chunk, r, d - 1],
            recv_sem=recv_in.at[chunk, r, d - 1],
            device_id={"tm": target},
            device_id_type=MESH,
        )

    def keep_in(chunk):
        return pltpu.make_async_copy(voltages_of(tm, chunk), got.at[tm, chunk], local_in.at[chunk])

    constants = [
        pltpu.make_async_copy(source_ref, held_ref, constant_sem.at[i])
        for i, (source_ref, held_ref) in enumerate(
            (
                (taps_any, taps_ref),
                (cos_any, cos_ref),
                (sin_any, sin_ref),
                (high_any, high_ref),
                (low_any, low_ref),
                (tile_a_any, tile_a_ref),
                (tile_b_any, tile_b_ref),
                (owner_any, owner_ref),
                (flags_any, flags_ref),
            )
        )
    ]

    def landing(refs, piece):
        start, end = piece
        if start >= inside:
            return refs[1], pl.ds(start - inside, end - start)
        return refs[0], pl.ds(start, end - start)

    def copy_out(chunk, b, k):
        to, target = device(k)
        start, end = pieces[chunk][b]
        ref, span = landing((own, own_last), (start, end))
        return pltpu.make_async_remote_copy(
            src_ref=made.at[target, chunk, pl.ds(start, end - start)],
            dst_ref=ref.at[me, chunk, span],
            send_sem=send_out.at[chunk, b, k - 1],
            recv_sem=recv_out.at[chunk, b, k - 1],
            device_id=to,
            device_id_type=MESH,
        )

    def keep_out(chunk, b):
        start, end = pieces[chunk][b]
        ref, span = landing((own, own_last), (start, end))
        return pltpu.make_async_copy(
            made.at[me, chunk, pl.ds(start, end - start)],
            ref.at[me, chunk, span],
            local_out.at[chunk, b],
        )

    def copy_pol(b):
        ref, span = landing((own, own_last), pieces[lately][b])
        target, _ = landing((other, other_last), pieces[lately][b])
        return pltpu.make_async_remote_copy(
            src_ref=ref.at[:, :, span],
            dst_ref=target.at[:, :, span],
            send_sem=send_pol.at[b],
            recv_sem=recv_pol.at[b],
            device_id={"pol": 1 - pol},
            device_id_type=MESH,
        )

    def send(chunk, b):
        for k in range(1, owners):
            copy_out(chunk, b, k).start()

    def await_out(chunk, b):
        keep_out(chunk, b).wait()
        for k in range(1, owners):
            copy_out(chunk, b, k).wait_recv()

    for r in range(2):
        for d in range(1, times):
            copy_in(0, r, d).start()
    for chunk in range(chunks):
        keep_in(chunk).start()
    for copy in constants:
        copy.start()
    for copy in constants:
        copy.wait()
    choose_tiles(tile_a_ref, tile_b_ref, owner_ref, flags_ref, pick, weight_ref, pol)
    for chunk in range(1, chunks):
        for r in range(2):
            for d in range(1, times):
                copy_in(chunk - 1, r, d).wait_send()
                copy_in(chunk, r, d).start()
    for chunk in range(chunks):
        keep_in(chunk).wait()
        for r in range(2):
            for d in range(1, times):
                copy_in(chunk, r, d).wait_recv()
        filter_and_transform(
            chunk, got, taps_ref, cos_ref, sin_ref, high_ref, low_ref, made, held, turned
        )
        for b in range(len(pieces[chunk])):
            keep_out(chunk, b).start()
            if chunk < lately or b < WINDOW:
                send(chunk, b)
            if chunk == 0 and b == 0:
                for r in range(2):
                    for d in range(1, times):
                        copy_in(lately, r, d).wait_send()
    for b, (start, end) in enumerate(pieces[lately]):
        await_out(lately, b)
        for chunk in range(lately):
            for early, piece in enumerate(pieces[chunk]):
                if start <= piece[0] < end:
                    await_out(chunk, early)
        copy_pol(b).start()
        if b + WINDOW < count:
            for k in range(1, owners):
                copy_out(lately, b, k).wait_send()
            send(lately, b + WINDOW)
        if end <= inside:
            copy_pol(b).wait_recv()
            for at in range(start // KEEP, end // KEEP):

                def one_unit(unit, carry, at=at):
                    correlate_unit(
                        unit, own, other, pol, pick, weight_ref, kept[at], at * KEEP
                    )
                    return carry

                lax.fori_loop(at * KEEP, (at + 1) * KEEP, one_unit, 0)
    for chunk in range(lately):
        for b in range(len(pieces[chunk])):
            for k in range(1, owners):
                copy_out(chunk, b, k).wait_send()
    for b, (start, _) in enumerate(pieces[lately]):
        if b + WINDOW >= count:
            for k in range(1, owners):
                copy_out(lately, b, k).wait_send()
        copy_pol(b).wait_send()
        if start >= inside:
            copy_pol(b).wait_recv()


def exchange(voltages, taps_filter, tile_a, tile_b, tile_owner, tile_flags, owners, times):
    _, stations, samples = voltages.shape
    taps, length = taps_filter.shape
    spectra_count = times * (samples // length)
    second = length // radix_first
    depth = AVG * spectra_count
    halves = radix_first // AVG
    chunks = stations // times // BLOCK
    units = second // owners
    inside = units - LAST
    tiles, width = tile_a.shape
    inner = np.arange(second)
    twist = 2.0 * np.pi / length * (np.arange(radix_first)[:, None] * inner[None, :])
    phase = 2.0 * np.pi / second * (inner[:, None] * inner[None, :] % second)
    c, s = np.cos(phase) / math.sqrt(length), np.sin(phase) / math.sqrt(length)
    matrix = np.block([[c, s], [-s, c]])
    high = matrix.astype(ml_dtypes.bfloat16)
    low = (matrix - high.astype(np.float64)).astype(ml_dtypes.bfloat16)
    early = [0, inside, units]
    late = [0, inside * 2 // 5, inside * 4 // 5, inside, units - 2, units - 1, units]
    count = max(len(early), len(late)) - 1
    shape = lambda count: (owners, chunks, count, halves, 2, BLOCK, depth)
    vmem = pl.BlockSpec(memory_space=pltpu.VMEM)
    anywhere = pl.BlockSpec(memory_space=pl.ANY)
    dma = pltpu.SemaphoreType.DMA
    far = lambda value: pltpu.with_memory_space_constraint(jnp.asarray(value), pltpu.HBM)
    return pl.pallas_call(
        functools.partial(exchange_kernel, early, late),
        in_specs=[pl.BlockSpec(memory_space=pltpu.HBM)] * 10,
        out_specs=[anywhere] * 2 + [vmem] * (2 + inside // KEEP),
        out_shape=[
            jax.ShapeDtypeStruct(shape(LAST), jnp.bfloat16),
            jax.ShapeDtypeStruct(shape(LAST), jnp.bfloat16),
            jax.ShapeDtypeStruct((CAP * 2 * width, owners * chunks * BLOCK), jnp.bfloat16),
            jax.ShapeDtypeStruct((CAP, 1, depth), jnp.bfloat16),
        ]
        + [
            jax.ShapeDtypeStruct((CAP, KEEP * halves, 2, 2, width, 2 * width), jnp.float32)
        ]
        * (inside // KEEP),
        scratch_shapes=[
            pltpu.VMEM((times, chunks, 2, BLOCK, samples), jnp.bfloat16),
            pltpu.VMEM(shape(units), jnp.bfloat16),
            pltpu.VMEM((2, BLOCK, spectra_count, length), jnp.float32),
            pltpu.VMEM((BLOCK, 2 * second, radix_first * spectra_count), jnp.float32),
            pltpu.VMEM(shape(inside), jnp.bfloat16),
            pltpu.VMEM(shape(inside), jnp.bfloat16),
            pltpu.VMEM((taps, length), jnp.float32),
            pltpu.VMEM((radix_first, second), jnp.float32),
            pltpu.VMEM((radix_first, second), jnp.float32),
            pltpu.VMEM((2 * second, 2 * second), jnp.bfloat16),
            pltpu.VMEM((2 * second, 2 * second), jnp.bfloat16),
            pltpu.VMEM((tiles, width), jnp.int32),
            pltpu.VMEM((tiles, width), jnp.int32),
            pltpu.VMEM((1, tiles), jnp.int32),
            pltpu.VMEM(tile_flags.shape, jnp.int32),
            dma((9,)),
            dma((chunks,)),
            dma((chunks, 2, times - 1)),
            dma((chunks, 2, times - 1)),
            dma((chunks, count)),
            dma((chunks, count, owners - 1)),
            dma((chunks, count, owners - 1)),
            dma((count,)),
            dma((count,)),
        ],
        cost_estimate=pl.CostEstimate(
            flops=16 * 10**9, bytes_accessed=32 * 2**20, transcendentals=0
        ),
        compiler_params=pltpu.CompilerParams(
            vmem_limit_bytes=24 * 2**20, collective_id=0, has_side_effects=True
        ),
    )(
        far(voltages),
        far(taps_filter),
        far(np.cos(twist).astype(np.float32)),
        far(np.sin(twist).astype(np.float32)),
        far(high),
        far(low),
        far(tile_a),
        far(tile_b),
        far(tile_owner.reshape(1, tiles)),
        far(tile_flags),
    )


def finish_kernel(own, other, pick, weight_ref, *refs):
    *kept, out_ref, block, kept_sem, block_sem = refs
    units, halves = own.shape[2:4]
    pol = lax.axis_index("pol")
    copies, inside = [], 0
    for i, vis in enumerate(kept):
        bands = vis.shape[1]
        copies.append(
            pltpu.make_async_copy(vis, out_ref.at[:, pl.ds(inside, bands)], kept_sem.at[i])
        )
        inside += bands
    for copy in copies:
        copy.start()
    for unit in range(units):
        correlate_unit(unit, own, other, pol, pick, weight_ref, block)
        copy = pltpu.make_async_copy(
            block.at[:, pl.ds(unit * halves, halves)],
            out_ref.at[:, pl.ds(inside + unit * halves, halves)],
            block_sem.at[unit],
        )
        copy.start()
        copies.append(copy)
    for copy in copies:
        copy.wait()


def finish(own, other, pick, weight, *kept):
    capacity = kept[0].shape[0]
    inside = sum(vis.shape[1] for vis in kept)
    sources, chunks, units, halves, _, block, depth = own.shape
    rest = kept[0].shape[2:]
    vmem = pl.BlockSpec(memory_space=pltpu.VMEM)
    return pl.pallas_call(
        finish_kernel,
        in_specs=[vmem] * (4 + len(kept)),
        out_specs=pl.BlockSpec(memory_space=pl.ANY),
        out_shape=jax.ShapeDtypeStruct((capacity, inside + units * halves) + rest, jnp.float32),
        scratch_shapes=[
            pltpu.VMEM((capacity, units * halves) + rest, jnp.float32),
            pltpu.SemaphoreType.DMA((len(kept),)),
            pltpu.SemaphoreType.DMA((units,)),
        ],
        compiler_params=pltpu.CompilerParams(vmem_limit_bytes=18 * 2**20),
    )(own, other, pick, weight, *kept)


def plain_spectra(blocks, taps_filter):
    _, time_count, share, samples = blocks.shape
    taps, length = taps_filter.shape
    frames = samples // length
    spectra_count = time_count * frames
    blocks = blocks.reshape(2, time_count, share, frames, length)
    blocks = blocks.transpose(0, 2, 1, 3, 4).reshape(2, share, spectra_count, length)
    extended = jnp.pad(blocks, ((0, 0), (0, 0), (taps - 1, 0), (0, 0)))
    filtered = jnp.zeros((2, share, spectra_count, length), jnp.float32)
    for tap_index in range(taps):
        start = taps - 1 - tap_index
        filtered = filtered + taps_filter[tap_index] * extended[
            :, :, start : start + spectra_count
        ].astype(jnp.float32)
    spectra = fourier(filtered.reshape(2, share * spectra_count, length)).astype(jnp.bfloat16)
    outgoing = spectra.reshape(
        2, share, spectra_count, length // radix_first, radix_first // AVG, AVG
    )
    return outgoing.transpose(3, 4, 0, 1, 5, 2).reshape(
        length // radix_first, radix_first // AVG, 2, share, AVG * spectra_count
    )


def correlate_kernel(place_ref, rows_ref, weight_ref, own_ref, other_ref, *rest):
    out_ref, pick, source = rest[-3:]
    sources, chunks, step, halves, parts, block, depth = own_ref.shape
    stations = sources * chunks * block
    capacity = out_ref.shape[0]
    width = out_ref.shape[4]

    @pl.when(pl.program_id(0) == 0)
    def _():
        columns = lax.broadcasted_iota(jnp.int32, pick.shape, 1)
        pick[...] = jnp.where(rows_ref[...] == columns, 1.0, 0.0).astype(jnp.bfloat16)

    for band in range(step * halves):
        for ref, polarisation in ((own_ref, place_ref[0]), (other_ref, 1 - place_ref[0])):
            at = pl.multiple_of(polarisation * (2 * depth), depth)
            source[band, :, pl.ds(at, 2 * depth)] = jnp.concatenate(
                [
                    ref[:, :, band // halves, band % halves, r].reshape(stations, depth)
                    for r in range(2)
                ],
                axis=-1,
            )
        picked = jnp.dot(pick[...], source[band], preferred_element_type=jnp.float32).astype(
            jnp.bfloat16
        )
        for slot in range(capacity):
            at = 2 * width * slot
            weight = weight_ref[slot]
            left = [
                picked[at : at + width, i * depth : (i + 1) * depth] * weight for i in range(4)
            ]
            other = picked[at + width : at + 2 * width]
            left_rows = jnp.concatenate(
                [
                    jnp.concatenate([left[0], left[1]], axis=-1),
                    jnp.concatenate([left[2], left[3]], axis=-1),
                    jnp.concatenate([left[1], -left[0]], axis=-1),
                    jnp.concatenate([left[3], -left[2]], axis=-1),
                ],
                axis=0,
            )
            right_rows = jnp.concatenate([other[:, : 2 * depth], other[:, 2 * depth :]], axis=0)
            result = lax.dot_general(
                left_rows,
                right_rows,
                (((1,), (1,)), ((), ())),
                preferred_element_type=jnp.float32,
            ) * (1.0 / depth)
            out_ref[slot, band] = result.reshape(2, 2, width, 2 * width)


def correlate(place, own, other, rows, weight, total_bands, first, earlier):
    sources, chunks, units, halves, parts, block, depth = own.shape
    width = rows.shape[1] // 2
    step = halves
    given = [] if earlier is None else [earlier]
    piece = pl.BlockSpec(
        (sources, chunks, 1, halves, parts, block, depth), lambda g: (0, 0, g, 0, 0, 0, 0)
    )
    return pl.pallas_call(
        correlate_kernel,
        grid=(units,),
        in_specs=[
            pl.BlockSpec(memory_space=pltpu.SMEM),
            pl.BlockSpec((CAP * 2 * width, 1), lambda g: (0, 0)),
            pl.BlockSpec((CAP, 1, depth), lambda g: (0, 0, 0)),
            piece,
            piece,
        ]
        + [pl.BlockSpec(memory_space=pl.ANY)] * len(given),
        out_specs=pl.BlockSpec(
            (CAP, step, 2, 2, width, 2 * width), lambda g: (0, g + first, 0, 0, 0, 0)
        ),
        out_shape=jax.ShapeDtypeStruct((CAP, total_bands, 2, 2, width, 2 * width), jnp.float32),
        scratch_shapes=[
            pltpu.VMEM((CAP * 2 * width, sources * chunks * block), jnp.bfloat16),
            pltpu.VMEM((step, sources * chunks * block, 4 * depth), jnp.bfloat16),
        ],
        input_output_aliases={5: 0} if given else {},
        cost_estimate=pl.CostEstimate(
            flops=units * 8 * 10**8, bytes_accessed=units * 2**21, transcendentals=0
        ),
        compiler_params=pltpu.CompilerParams(vmem_limit_bytes=48 * 2**20),
    )(
        place,
        rows.reshape(CAP * 2 * width, 1),
        weight.astype(jnp.bfloat16),
        own,
        other,
        *given,
    )


def on_device(voltages, taps_filter, tile_a, tile_b, tile_owner, tile_flags):
    taps, length = taps_filter.shape
    stations = voltages.shape[2]
    frames = voltages.shape[3] // length
    chan_count = lax.axis_size("chan")
    time_count = lax.axis_size("tm")
    spectra_count = time_count * frames
    share = stations // time_count
    owners = chan_count * time_count
    bands = length // (owners * AVG)
    halves = radix_first // AVG

    if share % BLOCK == 0:
        results = exchange(
            voltages[:, 0],
            taps_filter,
            tile_a,
            tile_b,
            tile_owner,
            tile_flags,
            owners,
            time_count,
        )
        return finish(*results)

    position = lax.axis_index("pol")
    held = tile_owner == position
    rank = jnp.cumsum(held.astype(jnp.int32)) - 1
    chosen = (
        (rank[None, :] == jnp.arange(CAP, dtype=jnp.int32)[:, None]) & held[None, :]
    ).astype(jnp.int32)
    pairs = jnp.concatenate([tile_a, tile_b], axis=1)
    rows = jnp.sum(chosen[:, :, None] * pairs[None], axis=1)[:, :, None]
    flags = jnp.sum(chosen[:, :, None] * tile_flags[None], axis=1)
    weight = jnp.tile(flags.astype(jnp.float32), (1, AVG))[:, None, :]
    place = position.reshape(1).astype(jnp.int32)
    swap = [(0, 1), (1, 0)]

    blocks = voltages.reshape(2, time_count, share, frames * length)
    blocks = lax.all_to_all(blocks, "tm", split_axis=1, concat_axis=1, tiled=True)
    spectra = plain_spectra(blocks, taps_filter)
    outgoing = spectra.reshape(owners, 1, bands // halves, halves, 2, share, AVG * spectra_count)
    moved = lax.all_to_all(outgoing, ("chan", "tm"), split_axis=0, concat_axis=0, tiled=True)
    other = lax.ppermute(moved, "pol", swap)
    return correlate(place, moved, other, rows, weight, bands, 0, None)


def solution(mesh):
    return jax.shard_map(
        on_device,
        mesh=mesh,
        in_specs=(P("grp", "pol", "chan", "tm"), P(), P(), P(), P(), P()),
        out_specs=P("pol", ("chan", "tm"), "grp", None, None, None),
        check_vma=False,
    )
```

```python
import functools
import math

import jax
import ml_dtypes
import numpy as np
import jax.numpy as jnp
from jax import lax
from jax.experimental import pallas as pl
from jax.experimental.pallas import tpu as pltpu
from jax.sharding import PartitionSpec as P

AVG = 8
CAP = 8

radix_first = 16
BLOCK = 16
LAST = 6
KEEP = 2
WINDOW = 3
MESH = pl.DeviceIdType.MESH


def fourier(filtered):
    length = filtered.shape[-1]
    second = length // radix_first
    mode = lax.Precision.HIGH
    grid = filtered.reshape(filtered.shape[:-1] + (radix_first, second))
    outer = jnp.arange(radix_first, dtype=jnp.int32)
    inner = jnp.arange(second, dtype=jnp.int32)
    phase_one = (
        2.0
        * math.pi
        / radix_first
        * (outer[:, None] * outer[None, :] % radix_first).astype(jnp.float32)
    )
    phase_twist = 2.0 * math.pi / length * (outer[:, None] * inner[None, :]).astype(jnp.float32)
    phase_two = (
        2.0 * math.pi / second * (inner[:, None] * inner[None, :] % second).astype(jnp.float32)
    )
    scale = 1.0 / math.sqrt(length)
    cos_one, sin_one = (jnp.cos(phase_one), jnp.sin(phase_one))
    cos_twist, sin_twist = (jnp.cos(phase_twist), jnp.sin(phase_twist))
    cos_two, sin_two = (jnp.cos(phase_two) * scale, jnp.sin(phase_two) * scale)
    one = jnp.stack([jnp.stack([cos_one, sin_one]), jnp.stack([-sin_one, cos_one])])
    two = jnp.stack([jnp.stack([cos_two, sin_two]), jnp.stack([-sin_two, cos_two])])
    section = jnp.einsum("qrfk,rnkj->qnfj", one, grid, precision=mode)
    turned = jnp.stack(
        [
            section[0] * cos_twist + section[1] * sin_twist,
            section[1] * cos_twist - section[0] * sin_twist,
        ]
    )
    return jnp.einsum("qrgj,rnfj->qngf", two, turned, precision=mode)


def times(value, angle):
    re, im = value
    if angle % 16 == 0:
        return re, im
    c, s = math.cos(2.0 * math.pi * angle / 16), math.sin(2.0 * math.pi * angle / 16)
    if angle % 16 == 4:
        return im, -re
    return re * c + im * s, im * c - re * s


def four(x):
    plus = [x[0][i] + x[2][i] for i in range(2)]
    minus = [x[0][i] - x[2][i] for i in range(2)]
    plus_odd = [x[1][i] + x[3][i] for i in range(2)]
    minus_odd = [x[1][i] - x[3][i] for i in range(2)]
    return [
        (plus[0] + plus_odd[0], plus[1] + plus_odd[1]),
        (minus[0] + minus_odd[1], minus[1] - minus_odd[0]),
        (plus[0] - plus_odd[0], plus[1] - plus_odd[1]),
        (minus[0] - minus_odd[1], minus[1] + minus_odd[0]),
    ]


def sixteen(x):
    inner = [four([x[4 * a + b] for a in range(4)]) for b in range(4)]
    result = [None] * 16
    for c in range(4):
        ends = four([times(inner[b][c], b * c) for b in range(4)])
        for d in range(4):
            result[c + 4 * d] = ends[d]
    return result


def filter_and_transform(chunk, got, taps_ref, cos_ref, sin_ref, high_ref, low_ref, made, held, turned):
    time_count, _, _, block, samples_count = got.shape
    taps, length = taps_ref.shape
    frames = samples_count // length
    spectra_count = time_count * frames
    second = length // radix_first
    depth = AVG * spectra_count
    owners, _, units = made.shape[:3]

    def filter_section(k1, carry):
        at = pl.multiple_of(k1 * second, second)
        rows = [taps_ref[m : m + 1, pl.ds(at, second)] for m in range(taps)]
        for r in range(2):
            samples = []
            for t in range(spectra_count):
                place = pl.multiple_of(k1 * second + (t % frames) * length, second)
                samples.append(
                    got[t // frames, chunk, r, :, pl.ds(place, second)].astype(jnp.float32)
                )
            filtered = []
            for t in range(spectra_count):
                total = rows[0] * samples[t]
                for m in range(1, min(taps, t + 1)):
                    total = total + rows[m] * samples[t - m]
                filtered.append(total)
            held[r, :, :, pl.ds(at, second)] = jnp.transpose(jnp.stack(filtered), (1, 0, 2))
        return carry

    lax.fori_loop(0, radix_first, filter_section, 0)

    def transform_station(s, carry):
        sections = [
            tuple(held[r, s, :, k1 * second : (k1 + 1) * second] for r in range(2))
            for k1 in range(radix_first)
        ]
        rows = []
        for f1, (re, im) in enumerate(sixteen(sections)):
            c, n = cos_ref[f1 : f1 + 1, :], sin_ref[f1 : f1 + 1, :]
            rows.append(jnp.concatenate([re * c + im * n, im * c - re * n], axis=-1))
        joined = jnp.concatenate(rows, axis=0)
        high = joined.astype(jnp.bfloat16)
        low = (joined - high.astype(jnp.float32)).astype(jnp.bfloat16)

        def product(matrix, data):
            return lax.dot_general(
                matrix, data, (((1,), (1,)), ((), ())), preferred_element_type=jnp.float32
            )

        turned[s] = (
            product(high_ref[...], high)
            + product(high_ref[...], low)
            + product(low_ref[...], high)
        )
        return carry

    lax.fori_loop(0, block, transform_station, 0)

    def place_channels(o, carry):
        at = pl.multiple_of(o * units, units)
        for q in range(2):
            for h in range(radix_first // AVG):
                part = turned[:, pl.ds(q * second + at, units), h * depth : (h + 1) * depth]
                made[o, chunk, :, h, q] = jnp.transpose(part, (1, 0, 2)).astype(jnp.bfloat16)
        return carry

    lax.fori_loop(0, owners, place_channels, 0)


def choose_tiles(tile_a_ref, tile_b_ref, owner_ref, flags_ref, pick, weight_ref, mine):
    tiles, width = tile_a_ref.shape
    capacity, _, depth = weight_ref.shape
    stations = pick.shape[1]
    held = jnp.where(owner_ref[...] == mine, 1.0, 0.0)
    at = lax.broadcasted_iota(jnp.int32, (tiles, tiles), 0)
    before = lax.broadcasted_iota(jnp.int32, (tiles, tiles), 1)
    held = jnp.broadcast_to(held, (tiles, tiles))
    count = jnp.sum(jnp.where(before <= at, held, 0.0), axis=1, keepdims=True)
    own = jnp.sum(jnp.where(before == at, held, 0.0), axis=1, keepdims=True)
    place = jnp.where(own > 0.5, count - 1.0, -1.0)
    pairs = jnp.concatenate([tile_a_ref[...], tile_b_ref[...]], axis=1).astype(jnp.float32)
    flags = jnp.concatenate(
        [flags_ref[...]] * (depth // flags_ref.shape[1]), axis=1
    ).astype(jnp.float32)
    column = lax.broadcasted_iota(jnp.int32, (2 * width, stations), 1).astype(jnp.float32)
    for slot in range(capacity):
        chosen = jnp.where(place == float(slot), 1.0, 0.0)
        rows = jnp.sum(chosen * pairs, axis=0, keepdims=True)
        rows = jnp.transpose(jnp.broadcast_to(rows, (2 * width, 2 * width)), (1, 0))
        rows = jnp.concatenate([rows] * (stations // (2 * width)), axis=1)
        pick[slot * 2 * width : (slot + 1) * 2 * width, :] = jnp.where(
            rows == column, 1.0, 0.0
        ).astype(jnp.bfloat16)
        weight = jnp.sum(chosen * flags, axis=0, keepdims=True) * (1.0 / depth)
        weight_ref[slot] = weight.astype(jnp.bfloat16)


def correlate_band(first, second, pick, weight_ref, out_ref, band):
    depth = weight_ref.shape[2]
    capacity = out_ref.shape[0]
    width = out_ref.shape[4]
    data = jnp.concatenate(first + second, axis=-1)
    picked = jnp.dot(pick[...], data, preferred_element_type=jnp.float32).astype(jnp.bfloat16)
    for slot in range(capacity):
        at = 2 * width * slot
        weight = weight_ref[slot]
        left = [picked[at : at + width, i * depth : (i + 1) * depth] * weight for i in range(4)]
        other = picked[at + width : at + 2 * width]
        left_rows = jnp.concatenate(
            [
                jnp.concatenate([left[0], left[1]], axis=-1),
                jnp.concatenate([left[2], left[3]], axis=-1),
                jnp.concatenate([left[1], -left[0]], axis=-1),
                jnp.concatenate([left[3], -left[2]], axis=-1),
            ],
            axis=0,
        )
        right_rows = jnp.concatenate([other[:, : 2 * depth], other[:, 2 * depth :]], axis=0)
        result = lax.dot_general(
            left_rows, right_rows, (((1,), (1,)), ((), ())), preferred_element_type=jnp.float32
        )
        out_ref[slot, band] = result.reshape(2, 2, width, 2 * width)


def correlate_unit(unit, own, other, flip, pick, weight_ref, out_ref, first_unit=0):
    sources, chunks, _, halves, parts, block, depth = own.shape
    stations = sources * chunks * block
    for half in range(halves):
        mine = [own[:, :, unit, half, r].reshape(stations, depth) for r in range(parts)]
        theirs = [other[:, :, unit, half, r].reshape(stations, depth) for r in range(parts)]
        first = [jnp.where(flip > 0, t, m) for m, t in zip(mine, theirs)]
        second = [jnp.where(flip > 0, m, t) for m, t in zip(mine, theirs)]
        band = (unit - first_unit) * halves + half
        correlate_band(first, second, pick, weight_ref, out_ref, band)


def exchange_kernel(early_cuts, late_cuts, *refs):
    (
        volt_ref,
        taps_any,
        cos_any,
        sin_any,
        high_any,
        low_any,
        tile_a_any,
        tile_b_any,
        owner_any,
        flags_any,
        own_last,
        other_last,
        pick,
        weight_ref,
        *refs,
    ) = refs
    kept, refs = refs[:-24], refs[-24:]
    (
        got,
        made,
        held,
        turned,
        own,
        other,
        taps_ref,
        cos_ref,
        sin_ref,
        high_ref,
        low_ref,
        tile_a_ref,
        tile_b_ref,
        owner_ref,
        flags_ref,
        constant_sem,
        local_in,
        send_in,
        recv_in,
        local_out,
        send_out,
        recv_out,
        send_pol,
        recv_pol,
    ) = refs
    times, chunks, _, block, _ = got.shape
    owners, _, units = made.shape[:3]
    inside = own.shape[2]
    chan, tm, pol = lax.axis_index("chan"), lax.axis_index("tm"), lax.axis_index("pol")
    me = chan * times + tm
    spans = lambda cuts: list(zip(cuts[:-1], cuts[1:]))
    pieces = [spans(early_cuts)] * (chunks - 1) + [spans(late_cuts)]
    lately = chunks - 1
    count = len(pieces[lately])

    def device(k):
        target = lax.rem(me + k, owners)
        return {"chan": target // times, "tm": lax.rem(target, times)}, target

    barrier = pltpu.get_barrier_semaphore()
    for k in range(1, owners):
        pl.semaphore_signal(barrier, inc=1, device_id=device(k)[0], device_id_type=MESH)
    pl.semaphore_signal(barrier, inc=1, device_id={"pol": 1 - pol}, device_id_type=MESH)
    pl.semaphore_wait(barrier, owners)

    def voltages_of(target, chunk):
        at = pl.multiple_of((target * chunks + chunk) * block, block)
        return volt_ref.at[:, pl.ds(at, block), :]

    def copy_in(chunk, r, d):
        target = lax.rem(tm + d, times)
        return pltpu.make_async_remote_copy(
            src_ref=voltages_of(target, chunk).at[r],
            dst_ref=got.at[tm, chunk, r],
            send_sem=send_in.at[chunk, r, d - 1],
            recv_sem=recv_in.at[chunk, r, d - 1],
            device_id={"tm": target},
            device_id_type=MESH,
        )

    def keep_in(chunk):
        return pltpu.make_async_copy(voltages_of(tm, chunk), got.at[tm, chunk], local_in.at[chunk])

    constants = [
        pltpu.make_async_copy(source_ref, held_ref, constant_sem.at[i])
        for i, (source_ref, held_ref) in enumerate(
            (
                (taps_any, taps_ref),
                (cos_any, cos_ref),
                (sin_any, sin_ref),
                (high_any, high_ref),
                (low_any, low_ref),
                (tile_a_any, tile_a_ref),
                (tile_b_any, tile_b_ref),
                (owner_any, owner_ref),
                (flags_any, flags_ref),
            )
        )
    ]

    def landing(refs, piece):
        start, end = piece
        if start >= inside:
            return refs[1], pl.ds(start - inside, end - start)
        return refs[0], pl.ds(start, end - start)

    def copy_out(chunk, b, k):
        to, target = device(k)
        start, end = pieces[chunk][b]
        ref, span = landing((own, own_last), (start, end))
        return pltpu.make_async_remote_copy(
            src_ref=made.at[target, chunk, pl.ds(start, end - start)],
            dst_ref=ref.at[me, chunk, span],
            send_sem=send_out.at[chunk, b, k - 1],
            recv_sem=recv_out.at[chunk, b, k - 1],
            device_id=to,
            device_id_type=MESH,
        )

    def keep_out(chunk, b):
        start, end = pieces[chunk][b]
        ref, span = landing((own, own_last), (start, end))
        return pltpu.make_async_copy(
            made.at[me, chunk, pl.ds(start, end - start)],
            ref.at[me, chunk, span],
            local_out.at[chunk, b],
        )

    def copy_pol(b):
        ref, span = landing((own, own_last), pieces[lately][b])
        target, _ = landing((other, other_last), pieces[lately][b])
        return pltpu.make_async_remote_copy(
            src_ref=ref.at[:, :, span],
            dst_ref=target.at[:, :, span],
            send_sem=send_pol.at[b],
            recv_sem=recv_pol.at[b],
            device_id={"pol": 1 - pol},
            device_id_type=MESH,
        )

    def send(chunk, b):
        for k in range(1, owners):
            copy_out(chunk, b, k).start()

    def await_out(chunk, b):
        keep_out(chunk, b).wait()
        for k in range(1, owners):
            copy_out(chunk, b, k).wait_recv()

    for r in range(2):
        for d in range(1, times):
            copy_in(0, r, d).start()
    for chunk in range(chunks):
        keep_in(chunk).start()
    for copy in constants:
        copy.start()
    for copy in constants:
        copy.wait()
    choose_tiles(tile_a_ref, tile_b_ref, owner_ref, flags_ref, pick, weight_ref, pol)
    for chunk in range(1, chunks):
        for r in range(2):
            for d in range(1, times):
                copy_in(chunk - 1, r, d).wait_send()
                copy_in(chunk, r, d).start()
    for chunk in range(chunks):
        keep_in(chunk).wait()
        for r in range(2):
            for d in range(1, times):
                copy_in(chunk, r, d).wait_recv()
        filter_and_transform(
            chunk, got, taps_ref, cos_ref, sin_ref, high_ref, low_ref, made, held, turned
        )
        for b in range(len(pieces[chunk])):
            keep_out(chunk, b).start()
            if chunk < lately or b < WINDOW:
                send(chunk, b)
            if chunk == 0 and b == 0:
                for r in range(2):
                    for d in range(1, times):
                        copy_in(lately, r, d).wait_send()
    for b, (start, end) in enumerate(pieces[lately]):
        await_out(lately, b)
        for chunk in range(lately):
            for early, piece in enumerate(pieces[chunk]):
                if start <= piece[0] < end:
                    await_out(chunk, early)
        copy_pol(b).start()
        if b + WINDOW < count:
            for k in range(1, owners):
                copy_out(lately, b, k).wait_send()
            send(lately, b + WINDOW)
        if end <= inside:
            copy_pol(b).wait_recv()
            for at in range(start // KEEP, end // KEEP):

                def one_unit(unit, carry, at=at):
                    correlate_unit(
                        unit, own, other, pol, pick, weight_ref, kept[at], at * KEEP
                    )
                    return carry

                lax.fori_loop(at * KEEP, (at + 1) * KEEP, one_unit, 0)
    for chunk in range(lately):
        for b in range(len(pieces[chunk])):
            for k in range(1, owners):
                copy_out(chunk, b, k).wait_send()
    for b, (start, _) in enumerate(pieces[lately]):
        if b + WINDOW >= count:
            for k in range(1, owners):
                copy_out(lately, b, k).wait_send()
        copy_pol(b).wait_send()
        if start >= inside:
            copy_pol(b).wait_recv()


def exchange(voltages, taps_filter, tile_a, tile_b, tile_owner, tile_flags, owners, times):
    _, stations, samples = voltages.shape
    taps, length = taps_filter.shape
    spectra_count = times * (samples // length)
    second = length // radix_first
    depth = AVG * spectra_count
    halves = radix_first // AVG
    chunks = stations // times // BLOCK
    units = second // owners
    inside = units - LAST
    tiles, width = tile_a.shape
    inner = np.arange(second)
    twist = 2.0 * np.pi / length * (np.arange(radix_first)[:, None] * inner[None, :])
    phase = 2.0 * np.pi / second * (inner[:, None] * inner[None, :] % second)
    c, s = np.cos(phase) / math.sqrt(length), np.sin(phase) / math.sqrt(length)
    matrix = np.block([[c, s], [-s, c]])
    high = matrix.astype(ml_dtypes.bfloat16)
    low = (matrix - high.astype(np.float64)).astype(ml_dtypes.bfloat16)
    early = [0, inside, units]
    late = [0, inside * 2 // 5, inside * 4 // 5, inside, units - 3, units - 1, units]
    count = max(len(early), len(late)) - 1
    shape = lambda count: (owners, chunks, count, halves, 2, BLOCK, depth)
    vmem = pl.BlockSpec(memory_space=pltpu.VMEM)
    anywhere = pl.BlockSpec(memory_space=pl.ANY)
    dma = pltpu.SemaphoreType.DMA
    far = lambda value: pltpu.with_memory_space_constraint(jnp.asarray(value), pltpu.HBM)
    return pl.pallas_call(
        functools.partial(exchange_kernel, early, late),
        in_specs=[pl.BlockSpec(memory_space=pltpu.HBM)] * 10,
        out_specs=[anywhere] * 2 + [vmem] * (2 + inside // KEEP),
        out_shape=[
            jax.ShapeDtypeStruct(shape(LAST), jnp.bfloat16),
            jax.ShapeDtypeStruct(shape(LAST), jnp.bfloat16),
            jax.ShapeDtypeStruct((CAP * 2 * width, owners * chunks * BLOCK), jnp.bfloat16),
            jax.ShapeDtypeStruct((CAP, 1, depth), jnp.bfloat16),
        ]
        + [
            jax.ShapeDtypeStruct((CAP, KEEP * halves, 2, 2, width, 2 * width), jnp.float32)
        ]
        * (inside // KEEP),
        scratch_shapes=[
            pltpu.VMEM((times, chunks, 2, BLOCK, samples), jnp.bfloat16),
            pltpu.VMEM(shape(units), jnp.bfloat16),
            pltpu.VMEM((2, BLOCK, spectra_count, length), jnp.float32),
            pltpu.VMEM((BLOCK, 2 * second, radix_first * spectra_count), jnp.float32),
            pltpu.VMEM(shape(inside), jnp.bfloat16),
            pltpu.VMEM(shape(inside), jnp.bfloat16),
            pltpu.VMEM((taps, length), jnp.float32),
            pltpu.VMEM((radix_first, second), jnp.float32),
            pltpu.VMEM((radix_first, second), jnp.float32),
            pltpu.VMEM((2 * second, 2 * second), jnp.bfloat16),
            pltpu.VMEM((2 * second, 2 * second), jnp.bfloat16),
            pltpu.VMEM((tiles, width), jnp.int32),
            pltpu.VMEM((tiles, width), jnp.int32),
            pltpu.VMEM((1, tiles), jnp.int32),
            pltpu.VMEM(tile_flags.shape, jnp.int32),
            dma((9,)),
            dma((chunks,)),
            dma((chunks, 2, times - 1)),
            dma((chunks, 2, times - 1)),
            dma((chunks, count)),
            dma((chunks, count, owners - 1)),
            dma((chunks, count, owners - 1)),
            dma((count,)),
            dma((count,)),
        ],
        cost_estimate=pl.CostEstimate(
            flops=16 * 10**9, bytes_accessed=32 * 2**20, transcendentals=0
        ),
        compiler_params=pltpu.CompilerParams(
            vmem_limit_bytes=24 * 2**20, collective_id=0, has_side_effects=True
        ),
    )(
        far(voltages),
        far(taps_filter),
        far(np.cos(twist).astype(np.float32)),
        far(np.sin(twist).astype(np.float32)),
        far(high),
        far(low),
        far(tile_a),
        far(tile_b),
        far(tile_owner.reshape(1, tiles)),
        far(tile_flags),
    )


def finish_kernel(own, other, pick, weight_ref, *refs):
    *kept, out_ref, block, kept_sem, block_sem = refs
    units, halves = own.shape[2:4]
    pol = lax.axis_index("pol")
    copies, inside = [], 0
    for i, vis in enumerate(kept):
        bands = vis.shape[1]
        copies.append(
            pltpu.make_async_copy(vis, out_ref.at[:, pl.ds(inside, bands)], kept_sem.at[i])
        )
        inside += bands
    for copy in copies:
        copy.start()
    for unit in range(units):
        correlate_unit(unit, own, other, pol, pick, weight_ref, block)
        copy = pltpu.make_async_copy(
            block.at[:, pl.ds(unit * halves, halves)],
            out_ref.at[:, pl.ds(inside + unit * halves, halves)],
            block_sem.at[unit],
        )
        copy.start()
        copies.append(copy)
    for copy in copies:
        copy.wait()


def finish(own, other, pick, weight, *kept):
    capacity = kept[0].shape[0]
    inside = sum(vis.shape[1] for vis in kept)
    sources, chunks, units, halves, _, block, depth = own.shape
    rest = kept[0].shape[2:]
    vmem = pl.BlockSpec(memory_space=pltpu.VMEM)
    return pl.pallas_call(
        finish_kernel,
        in_specs=[vmem] * (4 + len(kept)),
        out_specs=pl.BlockSpec(memory_space=pl.ANY),
        out_shape=jax.ShapeDtypeStruct((capacity, inside + units * halves) + rest, jnp.float32),
        scratch_shapes=[
            pltpu.VMEM((capacity, units * halves) + rest, jnp.float32),
            pltpu.SemaphoreType.DMA((len(kept),)),
            pltpu.SemaphoreType.DMA((units,)),
        ],
        compiler_params=pltpu.CompilerParams(vmem_limit_bytes=18 * 2**20),
    )(own, other, pick, weight, *kept)


def plain_spectra(blocks, taps_filter):
    _, time_count, share, samples = blocks.shape
    taps, length = taps_filter.shape
    frames = samples // length
    spectra_count = time_count * frames
    blocks = blocks.reshape(2, time_count, share, frames, length)
    blocks = blocks.transpose(0, 2, 1, 3, 4).reshape(2, share, spectra_count, length)
    extended = jnp.pad(blocks, ((0, 0), (0, 0), (taps - 1, 0), (0, 0)))
    filtered = jnp.zeros((2, share, spectra_count, length), jnp.float32)
    for tap_index in range(taps):
        start = taps - 1 - tap_index
        filtered = filtered + taps_filter[tap_index] * extended[
            :, :, start : start + spectra_count
        ].astype(jnp.float32)
    spectra = fourier(filtered.reshape(2, share * spectra_count, length)).astype(jnp.bfloat16)
    outgoing = spectra.reshape(
        2, share, spectra_count, length // radix_first, radix_first // AVG, AVG
    )
    return outgoing.transpose(3, 4, 0, 1, 5, 2).reshape(
        length // radix_first, radix_first // AVG, 2, share, AVG * spectra_count
    )


def correlate_kernel(place_ref, rows_ref, weight_ref, own_ref, other_ref, *rest):
    out_ref, pick, source = rest[-3:]
    sources, chunks, step, halves, parts, block, depth = own_ref.shape
    stations = sources * chunks * block
    capacity = out_ref.shape[0]
    width = out_ref.shape[4]

    @pl.when(pl.program_id(0) == 0)
    def _():
        columns = lax.broadcasted_iota(jnp.int32, pick.shape, 1)
        pick[...] = jnp.where(rows_ref[...] == columns, 1.0, 0.0).astype(jnp.bfloat16)

    for band in range(step * halves):
        for ref, polarisation in ((own_ref, place_ref[0]), (other_ref, 1 - place_ref[0])):
            at = pl.multiple_of(polarisation * (2 * depth), depth)
            source[band, :, pl.ds(at, 2 * depth)] = jnp.concatenate(
                [
                    ref[:, :, band // halves, band % halves, r].reshape(stations, depth)
                    for r in range(2)
                ],
                axis=-1,
            )
        picked = jnp.dot(pick[...], source[band], preferred_element_type=jnp.float32).astype(
            jnp.bfloat16
        )
        for slot in range(capacity):
            at = 2 * width * slot
            weight = weight_ref[slot]
            left = [
                picked[at : at + width, i * depth : (i + 1) * depth] * weight for i in range(4)
            ]
            other = picked[at + width : at + 2 * width]
            left_rows = jnp.concatenate(
                [
                    jnp.concatenate([left[0], left[1]], axis=-1),
                    jnp.concatenate([left[2], left[3]], axis=-1),
                    jnp.concatenate([left[1], -left[0]], axis=-1),
                    jnp.concatenate([left[3], -left[2]], axis=-1),
                ],
                axis=0,
            )
            right_rows = jnp.concatenate([other[:, : 2 * depth], other[:, 2 * depth :]], axis=0)
            result = lax.dot_general(
                left_rows,
                right_rows,
                (((1,), (1,)), ((), ())),
                preferred_element_type=jnp.float32,
            ) * (1.0 / depth)
            out_ref[slot, band] = result.reshape(2, 2, width, 2 * width)


def correlate(place, own, other, rows, weight, total_bands, first, earlier):
    sources, chunks, units, halves, parts, block, depth = own.shape
    width = rows.shape[1] // 2
    step = halves
    given = [] if earlier is None else [earlier]
    piece = pl.BlockSpec(
        (sources, chunks, 1, halves, parts, block, depth), lambda g: (0, 0, g, 0, 0, 0, 0)
    )
    return pl.pallas_call(
        correlate_kernel,
        grid=(units,),
        in_specs=[
            pl.BlockSpec(memory_space=pltpu.SMEM),
            pl.BlockSpec((CAP * 2 * width, 1), lambda g: (0, 0)),
            pl.BlockSpec((CAP, 1, depth), lambda g: (0, 0, 0)),
            piece,
            piece,
        ]
        + [pl.BlockSpec(memory_space=pl.ANY)] * len(given),
        out_specs=pl.BlockSpec(
            (CAP, step, 2, 2, width, 2 * width), lambda g: (0, g + first, 0, 0, 0, 0)
        ),
        out_shape=jax.ShapeDtypeStruct((CAP, total_bands, 2, 2, width, 2 * width), jnp.float32),
        scratch_shapes=[
            pltpu.VMEM((CAP * 2 * width, sources * chunks * block), jnp.bfloat16),
            pltpu.VMEM((step, sources * chunks * block, 4 * depth), jnp.bfloat16),
        ],
        input_output_aliases={5: 0} if given else {},
        cost_estimate=pl.CostEstimate(
            flops=units * 8 * 10**8, bytes_accessed=units * 2**21, transcendentals=0
        ),
        compiler_params=pltpu.CompilerParams(vmem_limit_bytes=48 * 2**20),
    )(
        place,
        rows.reshape(CAP * 2 * width, 1),
        weight.astype(jnp.bfloat16),
        own,
        other,
        *given,
    )


def on_device(voltages, taps_filter, tile_a, tile_b, tile_owner, tile_flags):
    taps, length = taps_filter.shape
    stations = voltages.shape[2]
    frames = voltages.shape[3] // length
    chan_count = lax.axis_size("chan")
    time_count = lax.axis_size("tm")
    spectra_count = time_count * frames
    share = stations // time_count
    owners = chan_count * time_count
    bands = length // (owners * AVG)
    halves = radix_first // AVG

    if share % BLOCK == 0:
        results = exchange(
            voltages[:, 0],
            taps_filter,
            tile_a,
            tile_b,
            tile_owner,
            tile_flags,
            owners,
            time_count,
        )
        return finish(*results)

    position = lax.axis_index("pol")
    held = tile_owner == position
    rank = jnp.cumsum(held.astype(jnp.int32)) - 1
    chosen = (
        (rank[None, :] == jnp.arange(CAP, dtype=jnp.int32)[:, None]) & held[None, :]
    ).astype(jnp.int32)
    pairs = jnp.concatenate([tile_a, tile_b], axis=1)
    rows = jnp.sum(chosen[:, :, None] * pairs[None], axis=1)[:, :, None]
    flags = jnp.sum(chosen[:, :, None] * tile_flags[None], axis=1)
    weight = jnp.tile(flags.astype(jnp.float32), (1, AVG))[:, None, :]
    place = position.reshape(1).astype(jnp.int32)
    swap = [(0, 1), (1, 0)]

    blocks = voltages.reshape(2, time_count, share, frames * length)
    blocks = lax.all_to_all(blocks, "tm", split_axis=1, concat_axis=1, tiled=True)
    spectra = plain_spectra(blocks, taps_filter)
    outgoing = spectra.reshape(owners, 1, bands // halves, halves, 2, share, AVG * spectra_count)
    moved = lax.all_to_all(outgoing, ("chan", "tm"), split_axis=0, concat_axis=0, tiled=True)
    other = lax.ppermute(moved, "pol", swap)
    return correlate(place, moved, other, rows, weight, bands, 0, None)


def solution(mesh):
    return jax.shard_map(
        on_device,
        mesh=mesh,
        in_specs=(P("grp", "pol", "chan", "tm"), P(), P(), P(), P(), P()),
        out_specs=P("pol", ("chan", "tm"), "grp", None, None, None),
        check_vma=False,
    )
```
